128 devices in a mesh: seq: 16 (over x, z), tp: 8 (over y, core).
Axes of the slice: x: 4, y: 4, z: 4, core: 2. Of those that a mesh axis runs over, the one named last changes fastest.
Arguments:
- inputs: bfloat16 [16384, 2048], P(('seq', 'tp')), may hold values from -6 to 6
- cotangent: bfloat16 [16384, 2048], P(('seq', 'tp')), may hold values from -6 to 6
- proj_in: float32 [4, 2048, 2048], P(None, 'seq', 'tp'), may hold values from -0.125 to 0.125
- proj_heads: float32 [2, 2048, 8], P(None, 'seq', 'tp'), may hold values from -0.125 to 0.125
- proj_out: float32 [2048, 2048], P('tp', 'seq'), may hold values from -0.1875 to 0.1875
- proj_mlp: float32 [2, 2048, 5632], P(None, 'seq', 'tp'), may hold values from -0.125 to 0.125
- proj_down: float32 [5632, 2048], P('tp', 'seq'), may hold values from -0.109375 to 0.109375
- vectors: float32 [28944], replicated, as said below
- first_in: float32 [4, 2048, 2048], P(None, 'seq', 'tp'), may hold values from -0.875 to 0.875
- first_heads: float32 [2, 2048, 8], P(None, 'seq', 'tp'), may hold values from -0.875 to 0.875
- first_out: float32 [2048, 2048], P('tp', 'seq'), may hold values from -0.875 to 0.875
- first_mlp: float32 [2, 2048, 5632], P(None, 'seq', 'tp'), may hold values from -0.875 to 0.875
- first_down: float32 [5632, 2048], P('tp', 'seq'), may hold values from -0.875 to 0.875
- first_vectors: float32 [28944], replicated, may hold values from -0.875 to 0.875
- second_in: float32 [4, 2048, 2048], P(None, 'seq', 'tp'), may hold values from 0.013 to 0.053
- second_heads: float32 [2, 2048, 8], P(None, 'seq', 'tp'), may hold values from 1 to 4
- second_out: float32 [2048, 2048], P('tp', 'seq'), may hold values from 0.013 to 0.053
- second_mlp: float32 [2, 2048, 5632], P(None, 'seq', 'tp'), may hold values from 0.013 to 0.053
- second_down: float32 [5632, 2048], P('tp', 'seq'), may hold values from 0.013 to 0.053
- second_vectors: float32 [28944], replicated, may hold values from 0.013 to 0.053
- average_in: float32 [4, 2048, 2048], P(None, 'seq', 'tp'), may hold values from -0.125 to 0.125
- average_heads: float32 [2, 2048, 8], P(None, 'seq', 'tp'), may hold values from -0.125 to 0.125
- average_out: float32 [2048, 2048], P('tp', 'seq'), may hold values from -0.1875 to 0.1875
- average_mlp: float32 [2, 2048, 5632], P(None, 'seq', 'tp'), may hold values from -0.125 to 0.125
- average_down: float32 [5632, 2048], P('tp', 'seq'), may hold values from -0.109375 to 0.109375
- average_vectors: float32 [28944], replicated, as said below
Outputs:
- outputs: bfloat16 [16384, 2048], P(('seq', 'tp'))
- input_grad: float32 [16384, 2048], P(('seq', 'tp'))
- grad_norm: float32 [], replicated
- new_proj_in: float32 [4, 2048, 2048], P(None, 'seq', 'tp')
- new_first_in: float32 [4, 2048, 2048], P(None, 'seq', 'tp')
- new_second_in: float32 [4, 2048, 2048], P(None, 'seq', 'tp')
- new_average_in: float32 [4, 2048, 2048], P(None, 'seq', 'tp')
- new_proj_heads: float32 [2, 2048, 8], P(None, 'seq', 'tp')
- new_first_heads: float32 [2, 2048, 8], P(None, 'seq', 'tp')
- new_second_heads: float32 [2, 2048, 8], P(None, 'seq', 'tp')
- new_average_heads: float32 [2, 2048, 8], P(None, 'seq', 'tp')
- new_proj_out: float32 [2048, 2048], P('tp', 'seq')
- new_first_out: float32 [2048, 2048], P('tp', 'seq')
- new_second_out: float32 [2048, 2048], P('tp', 'seq')
- new_average_out: float32 [2048, 2048], P('tp', 'seq')
- new_proj_mlp: float32 [2, 2048, 5632], P(None, 'seq', 'tp')
- new_first_mlp: float32 [2, 2048, 5632], P(None, 'seq', 'tp')
- new_second_mlp: float32 [2, 2048, 5632], P(None, 'seq', 'tp')
- new_average_mlp: float32 [2, 2048, 5632], P(None, 'seq', 'tp')
- new_proj_down: float32 [5632, 2048], P('tp', 'seq')
- new_first_down: float32 [5632, 2048], P('tp', 'seq')
- new_second_down: float32 [5632, 2048], P('tp', 'seq')
- new_average_down: float32 [5632, 2048], P('tp', 'seq')
- new_vectors: float32 [28944], replicated
- new_first_vectors: float32 [28944], replicated
- new_second_vectors: float32 [28944], replicated
- new_average_vectors: float32 [28944], replicated
The draws below stay inside these ranges and needn't reach their ends.
Inputs may be any that keep to these rules, and one draw needn't show every extreme that they name: `vectors`: entries [0, 2048) are the first norm's gain, [2048, 4096) the second norm's gain, the next 256 the output norm's gain, then 8 log decay rates, 8 decay biases and 24576 convolution taps laid out as [3, 4, 2048]. `average_vectors`: laid out as vectors.
All inputs are finite; a program needn't handle non-finite values.
Results may differ from the reference program's by a relative error of at most 0.024.
Values may be sent and summed in bfloat16 or wider, within the bound.
No kernel may reach another device: no remote copies, remote signals or barrier semaphores. Data moves between devices by JAX's collectives and lax.ppermute only.
A program may use at most 192 MiB of HBM per device.

```python
import math
import jax
import jax.numpy as jnp
from jax import lax

D = 2048
H = 8
DK = 256
FF = 5632
CONV = 4
BLOCK = 64
STEP = 7
KEYS = 2048
TOKENS = 16384
NSMALL = 28944
NPARAM = 55636240


def vector_values(key, spread, slow_end, fast_end):
    keys_list = jax.random.split(key, 6)
    placing = jnp.arange(D, dtype=jnp.float32) / D - 0.5
    gain_one = jnp.exp(spread * placing) * jax.random.uniform(keys_list[0], (D,), jnp.float32, 0.8, 1.2)
    gain_two = jnp.exp(spread * placing) * jax.random.uniform(keys_list[1], (D,), jnp.float32, 0.8, 1.2)
    gain_out = jax.random.uniform(keys_list[2], (DK,), jnp.float32, 0.7, 1.3)
    log_rate = jax.random.uniform(keys_list[3], (H,), jnp.float32, slow_end, fast_end)
    rate_bias = jax.random.uniform(keys_list[4], (H,), jnp.float32, -1.0, 1.0)
    conv_taps = 0.5 * jax.random.normal(keys_list[5], (3 * CONV * KEYS,), jnp.float32)
    return jnp.concatenate([gain_one, gain_two, gain_out, log_rate, rate_bias, conv_taps])


def draw_vectors(key, part):
    key = jax.random.fold_in(key, 11)
    return vector_values(key, math.log(3.0), math.log(1.0 / TOKENS), math.log(0.05))


def draw_average_vectors(key, part):
    key = jax.random.fold_in(key, 12)
    return vector_values(key, math.log(3.0), math.log(1.0 / TOKENS), math.log(0.05))


def block_levels(own_key, dims, pieces, low, largest):
    loudness = 1.0
    for dim, blocks in pieces:
        draws = jax.random.uniform(jax.random.fold_in(jax.random.fold_in(own_key, 6), dim), (blocks,), jnp.float32, low / len(pieces), largest / len(pieces))
        loudness = loudness * jnp.repeat(jnp.exp(draws), dims[dim] // blocks).reshape((-1,) + (1,) * (len(dims) - 1 - dim))
    return loudness


def centred(own_key, shape, deviation, reach, cuts=(), kind=jnp.bfloat16):
    factor_of = block_levels(own_key, shape, cuts, -0.22, 0.18) if cuts else 1.0
    array = jax.random.normal(own_key, shape, jnp.float32) * deviation * factor_of
    return jnp.minimum(jnp.maximum(array, -reach), reach).astype(kind)


def setup_inputs(seed: int = 0) -> dict:
    arg_keys = jax.random.split(jax.random.key(seed), 27)
    inputs = centred(arg_keys[0], (TOKENS, D), 1.0, 6.0, ((0, 128),))
    cotangent = centred(arg_keys[1], (TOKENS, D), 1.0, 6.0, ((0, 128),))
    proj_in = centred(arg_keys[2], (4, D, KEYS), D ** -0.5, 0.125, ((1, 16), (2, 8)), jnp.float32)
    proj_heads = centred(arg_keys[3], (2, D, H), D ** -0.5, 0.125, ((1, 16), (2, 8)), jnp.float32)
    proj_out = centred(arg_keys[4], (KEYS, D), (KEYS // 2) ** -0.5, 0.1875, ((0, 8), (1, 16)), jnp.float32)
    proj_mlp = centred(arg_keys[5], (2, D, FF), D ** -0.5, 0.125, ((1, 16), (2, 8)), jnp.float32)
    proj_down = centred(arg_keys[6], (FF, D), (FF // 2) ** -0.5, 0.109375, ((0, 8), (1, 16)), jnp.float32)
    vectors = draw_vectors(jax.random.fold_in(arg_keys[26], 71), 0)
    first_in = centred(arg_keys[8], (4, D, KEYS), 0.055, 0.875, ((1, 16), (2, 8)), jnp.float32)
    first_heads = centred(arg_keys[9], (2, D, H), 0.055, 0.875, ((1, 16), (2, 8)), jnp.float32)
    first_out = centred(arg_keys[10], (KEYS, D), 0.055, 0.875, ((0, 8), (1, 16)), jnp.float32)
    first_mlp = centred(arg_keys[11], (2, D, FF), 0.055, 0.875, ((1, 16), (2, 8)), jnp.float32)
    first_down = centred(arg_keys[12], (FF, D), 0.055, 0.875, ((0, 8), (1, 16)), jnp.float32)
    first_vectors = centred(arg_keys[13], (NSMALL,), 0.055, 0.875, (), jnp.float32)
    second_in = jnp.clip(jnp.exp(math.log(0.053) - 1.40534252 * jax.random.uniform(arg_keys[14], (4, D, KEYS), jnp.float32) ** block_levels(arg_keys[14], (4, D, KEYS), ((1, 16), (2, 8)), -0.2, 0.2)), 0.013, 0.053)
    second_heads = jnp.clip(jnp.exp(math.log(4.0) - 1.3862944 * jax.random.uniform(arg_keys[15], (2, D, H), jnp.float32) ** block_levels(arg_keys[15], (2, D, H), ((1, 16), (2, 8)), -0.2, 0.2)), 1.0, 4.0)
    second_out = jnp.clip(jnp.exp(math.log(0.053) - 1.40534252 * jax.random.uniform(arg_keys[16], (KEYS, D), jnp.float32) ** block_levels(arg_keys[16], (KEYS, D), ((0, 8), (1, 16)), -0.2, 0.2)), 0.013, 0.053)
    second_mlp = jnp.clip(jnp.exp(math.log(0.053) - 1.40534252 * jax.random.uniform(arg_keys[17], (2, D, FF), jnp.float32) ** block_levels(arg_keys[17], (2, D, FF), ((1, 16), (2, 8)), -0.2, 0.2)), 0.013, 0.053)
    second_down = jnp.clip(jnp.exp(math.log(0.053) - 1.40534252 * jax.random.uniform(arg_keys[18], (FF, D), jnp.float32) ** block_levels(arg_keys[18], (FF, D), ((0, 8), (1, 16)), -0.2, 0.2)), 0.013, 0.053)
    second_vectors = jnp.clip(jnp.exp(jax.random.uniform(arg_keys[19], (NSMALL,), jnp.float32, math.log(0.013), math.log(0.053))), 0.013, 0.053)
    average_in = centred(arg_keys[20], (4, D, KEYS), D ** -0.5, 0.125, ((1, 16), (2, 8)), jnp.float32)
    average_heads = centred(arg_keys[21], (2, D, H), D ** -0.5, 0.125, ((1, 16), (2, 8)), jnp.float32)
    average_out = centred(arg_keys[22], (KEYS, D), (KEYS // 2) ** -0.5, 0.1875, ((0, 8), (1, 16)), jnp.float32)
    average_mlp = centred(arg_keys[23], (2, D, FF), D ** -0.5, 0.125, ((1, 16), (2, 8)), jnp.float32)
    average_down = centred(arg_keys[24], (FF, D), (FF // 2) ** -0.5, 0.109375, ((0, 8), (1, 16)), jnp.float32)
    average_vectors = draw_average_vectors(jax.random.fold_in(arg_keys[26], 71), 0)
    return {"inputs": inputs, "cotangent": cotangent, "proj_in": proj_in, "proj_heads": proj_heads, "proj_out": proj_out, "proj_mlp": proj_mlp, "proj_down": proj_down, "vectors": vectors, "first_in": first_in, "first_heads": first_heads, "first_out": first_out, "first_mlp": first_mlp, "first_down": first_down, "first_vectors": first_vectors, "second_in": second_in, "second_heads": second_heads, "second_out": second_out, "second_mlp": second_mlp, "second_down": second_down, "second_vectors": second_vectors, "average_in": average_in, "average_heads": average_heads, "average_out": average_out, "average_mlp": average_mlp, "average_down": average_down, "average_vectors": average_vectors}


highest = lax.Precision.HIGHEST
beta_one = 0.9
beta_two = 0.95
adam_eps = 1e-08
ema_decay = 0.6
rate_matrix = 0.02
rate_vector = 0.5
decay_matrix = 0.1

@jax.custom_vjp
def low(v):
    return lax.optimization_barrier(v.astype(jnp.bfloat16)).astype(jnp.float32)

@jax.custom_vjp
def low_back(v):
    return v

def low_keep(v):
    return (low(v), None)

def low_pass(kept, grad):
    return (grad,)

def back_keep(v):
    return (v, None)

def back_low(kept, grad):
    return (low(grad),)
low.defvjp(low_keep, low_pass)
low_back.defvjp(back_keep, back_low)

def split_vectors(vectors):
    offset = 2 * D + DK
    gain_one = vectors[:D]
    gain_two = vectors[D:2 * D]
    gain_out = vectors[2 * D:offset]
    log_rate = vectors[offset:offset + H]
    rate_bias = vectors[offset + H:offset + 2 * H]
    conv_taps = vectors[offset + 2 * H:].reshape(3, CONV, KEYS)
    return (gain_one, gain_two, gain_out, log_rate, rate_bias, conv_taps)

def norm_rows(values, gain_row):
    return values * lax.rsqrt(lax.optimization_barrier(jnp.mean(values * values, -1, keepdims=True)) + 1e-05) * gain_row

def activate(conv_out):
    activated = jax.nn.silu(conv_out).reshape(conv_out.shape[0], 3, -1, DK)
    query_rows = activated[:, 0] * lax.rsqrt(lax.optimization_barrier(jnp.sum(activated[:, 0] * activated[:, 0], -1, keepdims=True)) + 1e-06) * DK ** (-0.5)
    key_rows = activated[:, 1] * lax.rsqrt(lax.optimization_barrier(jnp.sum(activated[:, 1] * activated[:, 1], -1, keepdims=True)) + 1e-06)
    return (query_rows, key_rows, activated[:, 2])

def group_step(states, blocks):
    query_rows, key_rows, value_rows, beta_gate, log_decay = blocks
    cumulative = jnp.cumsum(log_decay, axis=0).T
    length = cumulative.shape[1]
    positions = jnp.arange(length)
    on_lower = positions[:, None] >= positions[None, :]
    strictly = positions[:, None] > positions[None, :]
    log_gap = cumulative[:, :, None] - cumulative[:, None, :]
    fading = jnp.where(on_lower, jnp.exp(jnp.where(on_lower, log_gap, 0.0)), 0.0)
    queries = jnp.transpose(query_rows, (1, 0, 2))
    keys_head = jnp.transpose(key_rows, (1, 0, 2))
    values_head = jnp.transpose(value_rows, (1, 0, 2))
    betas_head = beta_gate.T
    key_key = jnp.einsum('htd,hsd->hts', keys_head, keys_head, precision=highest)
    query_key = jnp.einsum('htd,hsd->hts', queries, keys_head, precision=highest)
    mixing = jnp.eye(length, dtype=jnp.float32) + jnp.where(strictly, betas_head[:, :, None] * fading * key_key, 0.0)
    growth = jnp.exp(cumulative)
    carried = jnp.einsum('htd,hdw->htw', keys_head, states, precision=highest)
    right_side = betas_head[:, :, None] * (values_head - growth[:, :, None] * carried)
    updates = lax.linalg.triangular_solve(mixing, right_side, left_side=True, lower=True, unit_diagonal=True)
    outputs_head = growth[:, :, None] * jnp.einsum('htd,hdw->htw', queries, states, precision=highest)
    outputs_head = outputs_head + jnp.einsum('hts,hsw->htw', fading * query_key, updates, precision=highest)
    totals = cumulative[:, -1]
    tail_fade = jnp.exp(totals[:, None] - cumulative)
    new_states = jnp.exp(totals)[:, None, None] * states + jnp.einsum('hsd,hsw->hdw', keys_head * tail_fade[:, :, None], updates, precision=highest)
    return (new_states, jnp.transpose(outputs_head, (1, 0, 2)))

def run_mixer(query_rows, key_rows, value_rows, beta_gate, log_decay):
    block_count = TOKENS // BLOCK
    blocks = tuple((member.reshape((block_count, BLOCK) + member.shape[1:]) for member in (query_rows, key_rows, value_rows, beta_gate, log_decay)))
    states = jnp.zeros((H, DK, DK), jnp.float32)
    last_state, block_out = lax.scan(jax.checkpoint(group_step), states, blocks)
    return block_out.reshape(TOKENS, H, DK)

def forward(inputs, proj_in, proj_heads, proj_out, proj_mlp, proj_down, vectors):
    gain_one, gain_two, gain_out, log_rate, rate_bias, conv_taps = split_vectors(vectors)
    normed = low(norm_rows(inputs, gain_one))
    projected = low_back(low(jnp.einsum('td,cdk->tck', normed, low(proj_in), precision=highest)))
    heads_in = low_back(low(jnp.einsum('td,cdh->tch', normed, low(proj_heads), precision=highest)))
    padded = jnp.concatenate([jnp.zeros((CONV - 1, 3, KEYS), jnp.float32), projected[:, :3]], 0)
    conv_out = low_back(sum((conv_taps[:, tap_index][None] * padded[tap_index:tap_index + TOKENS] for tap_index in range(CONV))))
    query_rows, key_rows, value_rows = activate(conv_out)
    beta_gate = jax.nn.sigmoid(heads_in[:, 1])
    log_decay = -jnp.exp(log_rate) * jax.nn.softplus(heads_in[:, 0] + rate_bias)
    mixed_out = run_mixer(low(query_rows), low(key_rows), low(value_rows), beta_gate, log_decay)
    unit_out = mixed_out * lax.rsqrt(lax.optimization_barrier(jnp.mean(mixed_out * mixed_out, -1, keepdims=True)) + 1e-05)
    gated_out = low((unit_out * gain_out).reshape(TOKENS, KEYS) * jax.nn.silu(projected[:, 3]))
    hidden = inputs + low_back(jnp.dot(gated_out, low(proj_out), precision=highest))
    normed_two = low(norm_rows(hidden, gain_two))
    gate_up = low_back(jnp.einsum('td,cdf->tcf', normed_two, low(proj_mlp), precision=highest))
    inner_act = low(jax.nn.silu(gate_up[:, 0]) * gate_up[:, 1])
    return hidden + jnp.dot(inner_act, low(proj_down), precision=highest)

def adam_step(weight, gradient, first_old, second_old, average_old, step_rate, decay_rate):
    first_new = beta_one * first_old + (1.0 - beta_one) * gradient
    second_new = beta_two * second_old + (1.0 - beta_two) * gradient * gradient
    direction = first_new / (1.0 - beta_one ** STEP) / (jnp.sqrt(second_new / (1.0 - beta_two ** STEP)) + adam_eps)
    weight_new = weight - step_rate * (direction + decay_rate * weight)
    average_new = ema_decay * average_old + (1.0 - ema_decay) * weight_new
    return (weight_new, first_new, second_new, average_new)

def reference(inputs, cotangent, proj_in, proj_heads, proj_out, proj_mlp, proj_down, vectors, first_in, first_heads, first_out, first_mlp, first_down, first_vectors, second_in, second_heads, second_out, second_mlp, second_down, second_vectors, average_in, average_heads, average_out, average_mlp, average_down, average_vectors):
    weights = (proj_in, proj_heads, proj_out, proj_mlp, proj_down, vectors)
    result, pull_back = jax.vjp(forward, inputs.astype(jnp.float32), *weights)
    gradients = pull_back(cotangent.astype(jnp.float32))
    input_grad = gradients[0]
    weight_grads = gradients[1:]
    grad_norm = jnp.sqrt(sum((jnp.sum(member * member) for member in weight_grads)))
    factor = jnp.minimum(1.0, 0.5 * math.sqrt(NPARAM) / (grad_norm + 1e-06))
    firsts = (first_in, first_heads, first_out, first_mlp, first_down, first_vectors)
    seconds = (second_in, second_heads, second_out, second_mlp, second_down, second_vectors)
    averages = (average_in, average_heads, average_out, average_mlp, average_down, average_vectors)
    rate_list = (rate_matrix,) * 5 + (rate_vector,)
    decays = (decay_matrix,) * 5 + (0.0,)
    updated = [adam_step(weights[index_at], factor * weight_grads[index_at], firsts[index_at], seconds[index_at], averages[index_at], rate_list[index_at], decays[index_at]) for index_at in range(6)]
    return (result.astype(jnp.bfloat16), input_grad, grad_norm, updated[0][0], updated[0][1], updated[0][2], updated[0][3], updated[1][0], updated[1][1], updated[1][2], updated[1][3], updated[2][0], updated[2][1], updated[2][2], updated[2][3], updated[3][0], updated[3][1], updated[3][2], updated[3][3], updated[4][0], updated[4][1], updated[4][2], updated[4][3], updated[5][0], updated[5][1], updated[5][2], updated[5][3])
```

```python
from functools import partial
import math

import jax
import jax.numpy as jnp
from jax import lax
from jax.sharding import PartitionSpec as P
from jax.experimental import pallas as pl
from jax.experimental.pallas import tpu as pltpu

DK = 256
CONV = 4
C = 256
HIGH = lax.Precision.HIGH
F32 = jnp.float32
BF16 = jnp.bfloat16


def mm(a, b, ca=1, cb=0, precision=None):
    return lax.dot_general(
        a, b, (((ca,), (cb,)), ((), ())), precision=precision, preferred_element_type=F32
    )


def mlow(a, b, ca=1, cb=0):
    return mm(a.astype(BF16), b.astype(BF16), ca, cb)


def mhigh(a, b, ca=1, cb=0):
    return mm(a, b, ca, cb, HIGH)


def sigmoid(v):
    return 1.0 / (1.0 + jnp.exp(-v))


def iotas(n):
    rows = lax.broadcasted_iota(jnp.int32, (n, n), 0)
    cols = lax.broadcasted_iota(jnp.int32, (n, n), 1)
    return rows, cols


def to_column(row, eye):
    return jnp.sum(jnp.where(eye, row, 0.0), 1, keepdims=True)


def to_row(column, eye):
    return jnp.sum(jnp.where(eye, column, 0.0), 0, keepdims=True)


def unit_inverse(strict_part, rows, cols):
    n = strict_part.shape[0]
    total = jnp.where(rows == cols, 1.0, 0.0) - jnp.where(
        (rows // 2 == cols // 2), strict_part, 0.0
    )
    size = 2
    while 2 * size <= n // 2:
        joint = (rows // (2 * size) == cols // (2 * size)) & (rows // size != cols // size)
        below = jnp.where(joint, strict_part, 0.0)
        total = total - mhigh(total, mhigh(below, total))
        size *= 2
    half = n // 2
    upper = total[:half, :half]
    lower = total[half:, half:]
    corner = -mhigh(lower, mhigh(strict_part[half:, :half], upper))
    return jnp.concatenate(
        [
            jnp.concatenate([upper, jnp.zeros((half, half), F32)], 1),
            jnp.concatenate([corner, lower], 1),
        ],
        0,
    )


def decay_terms(decay_row, rows, cols):
    lower = rows >= cols
    sums = mm(
        jnp.broadcast_to(decay_row, (8, C)),
        jnp.where(rows <= cols, 1.0, 0.0),
        precision=lax.Precision.HIGHEST,
    )[:1]
    column = to_column(sums, rows == cols)
    gap = jnp.where(lower, column - sums, 0.0)
    fading = jnp.where(lower, jnp.exp(gap), 0.0)
    return column, fading


def conv_rows(raw_ref, padded, taps_ref, rim_ref, step, width):
    @pl.when(step == 0)
    def _():
        padded[0:8] = rim_ref[...]

    @pl.when(step > 0)
    def _():
        padded[0:8] = padded[C : C + 8]

    padded[8 : C + 8] = raw_ref[...].astype(F32)
    return sum(taps_ref[j : j + 1, :] * padded[5 + j : 5 + j + C] for j in range(CONV))


def activated(conv_out):
    act = conv_out * sigmoid(conv_out)
    q, k, v = act[:, :DK], act[:, DK : 2 * DK], act[:, 2 * DK :]
    inv_q = lax.rsqrt(jnp.sum(q * q, 1, keepdims=True) + 1e-06)
    inv_k = lax.rsqrt(jnp.sum(k * k, 1, keepdims=True) + 1e-06)
    return q, k, v, inv_q, inv_k


def forward_kernel(
    raw_ref, rim_ref, taps_ref, decay_ref, beta_ref,
    q_ref, k_ref, conv_ref, x_ref, p_ref, vt_ref, kt_ref, qt_ref, ol_ref, a_ref, b_ref, total_ref,
    padded,
):
    step = pl.program_id(0)
    conv_out = conv_rows(raw_ref, padded, taps_ref, rim_ref, step, 3 * DK)
    conv_ref[...] = conv_out
    q, k, v, inv_q, inv_k = activated(conv_out)
    q = (q * inv_q * DK**-0.5).astype(BF16)
    k = (k * inv_k).astype(BF16)
    v = v.astype(BF16).astype(F32)
    q_ref[...] = q
    k_ref[...] = k
    rows, cols = iotas(C)
    eye = rows == cols
    column, fading = decay_terms(decay_ref[0], rows, cols)
    beta = to_column(beta_ref[0], eye)
    kf = k.astype(F32)
    strict = jnp.where(rows > cols, beta * fading * mm(k, k, 1, 1), 0.0)
    inverse = unit_inverse(strict, rows, cols)
    growth = jnp.exp(column)
    last = column[C - 1 : C, :]
    right = jnp.concatenate([beta * v, (beta * growth) * kf], 1)
    both = mhigh(inverse, right)
    p = (fading * mm(q, k, 1, 1)).astype(BF16)
    shared = both.astype(BF16)
    seen = mm(p, shared)
    ol_ref[...] = seen[:, :DK]
    qt_ref[...] = (growth * q.astype(F32) - seen[:, DK:]).astype(BF16)
    kd = kf * jnp.exp(last - column)
    ends = mhigh(kd, both, 0, 0)
    a = jnp.where(eye, jnp.exp(last), 0.0) - ends[:, DK:]
    b = ends[:, :DK]
    x_ref[...] = inverse.astype(BF16)
    p_ref[...] = p
    vt_ref[...] = both[:, :DK]
    kt_ref[...] = shared[:, DK:]
    a_ref[0] = a
    b_ref[0] = b

    @pl.when(step == 0)
    def _():
        total_ref[...] = jnp.concatenate([b, a], 1)

    @pl.when(step > 0)
    def _():
        moved = mhigh(a, total_ref[...])
        total_ref[...] = jnp.concatenate([moved[:, :DK] + b, moved[:, DK:]], 1)


def local_forward(raw, rim, taps, decay, beta):
    tokens = raw.shape[0]
    n = tokens // C
    tile = lambda width: pl.BlockSpec((C, width), lambda i: (i, 0))
    whole = lambda shape: pl.BlockSpec(shape, lambda i: (0,) * len(shape))
    line = pl.BlockSpec((1, 1, C), lambda i: (i, 0, 0))
    square = pl.BlockSpec((1, DK, DK), lambda i: (i, 0, 0))
    struct = jax.ShapeDtypeStruct
    return pl.pallas_call(
        forward_kernel,
        grid=(n,),
        in_specs=[tile(3 * DK), whole((8, 3 * DK)), whole((CONV, 3 * DK)), line, line],
        out_specs=[tile(DK), tile(DK), tile(3 * DK)] + [tile(C)] * 2 + [tile(DK)] * 4
        + [square, square, whole((DK, 2 * DK))],
        out_shape=[
            struct((tokens, DK), BF16),
            struct((tokens, DK), BF16),
            struct((tokens, 3 * DK), F32),
            struct((tokens, C), BF16),
            struct((tokens, C), BF16),
            struct((tokens, DK), F32),
            struct((tokens, DK), BF16),
            struct((tokens, DK), BF16),
            struct((tokens, DK), F32),
            struct((n, DK, DK), F32),
            struct((n, DK, DK), F32),
            struct((DK, 2 * DK), F32),
        ],
        scratch_shapes=[pltpu.VMEM((C + 8, 3 * DK), F32)],
        compiler_params=pltpu.CompilerParams(vmem_limit_bytes=48 * 2**20),
        name="local_forward",
    )(raw, rim, taps, decay, beta)


def output_kernel(state_ref, a_ref, b_ref, qt_ref, ol_ref, gate_ref, gain_ref, u_ref, states_ref, o_ref, held):
    step = pl.program_id(0)

    @pl.when(step == 0)
    def _():
        held[...] = state_ref[...]

    state = held[...]
    states_ref[0] = state.astype(BF16)
    low = state.astype(BF16)
    o = mm(qt_ref[...], low) + ol_ref[...]
    o_ref[...] = o
    inverse = lax.rsqrt(jnp.mean(o * o, 1, keepdims=True) + 1e-05)
    gate = gate_ref[...].astype(F32)
    u_ref[...] = (o * inverse * gain_ref[...] * (gate * sigmoid(gate))).astype(BF16)
    held[...] = mhigh(a_ref[0], state) + b_ref[0]


def mixer_output(state, a, b, qt, ol, gate, gain):
    tokens = qt.shape[0]
    n = tokens // C
    tile = pl.BlockSpec((C, DK), lambda i: (i, 0))
    square = pl.BlockSpec((1, DK, DK), lambda i: (i, 0, 0))
    whole = lambda shape: pl.BlockSpec(shape, lambda i: (0,) * len(shape))
    struct = jax.ShapeDtypeStruct
    return pl.pallas_call(
        output_kernel,
        grid=(n,),
        in_specs=[whole((DK, DK)), square, square, tile, tile,
                  pl.BlockSpec((C, DK), lambda i: (i, gate[1])), whole((1, DK))],
        out_specs=[tile, square, tile],
        out_shape=[struct((tokens, DK), BF16), struct((n, DK, DK), BF16), struct((tokens, DK), F32)],
        scratch_shapes=[pltpu.VMEM((DK, DK), F32)],
        compiler_params=pltpu.CompilerParams(vmem_limit_bytes=48 * 2**20),
        name="mixer_output",
    )(state, a, b, qt, ol, gate[0], gain)


def output_back_kernel(
    du_ref, o_ref, gate_ref, gain_ref, a_ref, qt_ref,
    do_ref, dgate_ref, dgain_ref, back_ref,
    held,
):
    step = pl.program_id(0)

    @pl.when(step == 0)
    def _():
        held[...] = jnp.zeros_like(held)
        dgain_ref[...] = jnp.zeros_like(dgain_ref)

    o = o_ref[...]
    inverse = lax.rsqrt(jnp.mean(o * o, 1, keepdims=True) + 1e-05)
    unit = o * inverse
    gain = gain_ref[...]
    gate = gate_ref[...].astype(F32)
    sig = sigmoid(gate)
    act = gate * sig
    du = du_ref[...]
    dgate_ref[...] = (du * (unit * gain) * sig * (1.0 + gate * (1.0 - sig))).astype(BF16)
    dm = du * act
    dgain_ref[...] += jnp.sum(dm * unit, 0, keepdims=True)
    e = dm * gain
    do = (inverse * (e - unit * jnp.mean(e * unit, 1, keepdims=True))).astype(BF16)
    do_ref[...] = do
    held[...] = mhigh(a_ref[0], held[...], 0, 0) + mm(qt_ref[...], do, 0, 0)
    back_ref[...] = held[...]


def output_back(du, o, gate, gain, a, qt):
    tokens = du.shape[0]
    n = tokens // C
    tile = pl.BlockSpec((C, DK), lambda i: (n - 1 - i, 0))
    square = pl.BlockSpec((1, DK, DK), lambda i: (n - 1 - i, 0, 0))
    whole = lambda shape: pl.BlockSpec(shape, lambda i: (0,) * len(shape))
    struct = jax.ShapeDtypeStruct
    return pl.pallas_call(
        output_back_kernel,
        grid=(n,),
        in_specs=[tile, tile, pl.BlockSpec((C, DK), lambda i: (n - 1 - i, gate[1])), whole((1, DK)), square, tile],
        out_specs=[tile, tile, whole((1, DK)), whole((DK, DK))],
        out_shape=[struct((tokens, DK), BF16), struct((tokens, DK), BF16), struct((1, DK), F32), struct((DK, DK), F32)],
        scratch_shapes=[pltpu.VMEM((DK, DK), F32)],
        compiler_params=pltpu.CompilerParams(vmem_limit_bytes=48 * 2**20),
        name="output_back",
    )(du, o, gate[0], gain, a, qt)


def silu_back(conv_out, grad):
    sig = sigmoid(conv_out)
    return grad * sig * (1.0 + conv_out * (1.0 - sig))


def backward_kernel(
    ends_ref, do_ref, q_ref, k_ref, conv_ref, x_ref, p_ref, vt_ref, kt_ref, qt_ref, a_ref, states_ref,
    decay_ref, beta_ref, raw_ref, before_ref, rim_ref, taps_ref,
    draw_ref, ddecay_ref, dbeta_ref, dtaps_ref, first_ref, last_ref,
    held, padded, dpad,
):
    step = pl.program_id(0)
    n = pl.num_programs(0)

    @pl.when(step == 0)
    def _():
        held[...] = ends_ref[...]
        dtaps_ref[...] = jnp.zeros_like(dtaps_ref)
        dpad[...] = jnp.zeros_like(dpad)

    rows, cols = iotas(C)
    eye = rows == cols
    column, fading = decay_terms(decay_ref[0], rows, cols)
    beta = to_column(beta_ref[0], eye)
    growth = jnp.exp(column)
    last = column[C - 1 : C, :]
    tail = jnp.exp(last - column)
    q, k, do, p, inverse, state = q_ref[...], k_ref[...], do_ref[...], p_ref[...], x_ref[...], states_ref[0]
    kf = k.astype(F32)
    qf = q.astype(F32)
    kd = (kf * tail).astype(BF16)
    dend = held[...]
    dlow = dend.astype(BF16)
    updates = vt_ref[...] - mm(kt_ref[...], state)
    ulow = updates.astype(BF16)
    dupdates = mm(p, do, 0, 0) + mm(kd, dlow)
    dright = mm(inverse, dupdates.astype(BF16), 0, 0)
    dlow_right = dright.astype(BF16)
    pair_q = jnp.where(rows >= cols, mm(do, ulow, 1, 1) * fading, 0.0).astype(BF16)
    pair_k = jnp.where(rows > cols, mm(dlow_right, ulow, 1, 1) * (-beta * fading), 0.0).astype(BF16)
    dq = growth * mm(do, state, 1, 1) + mm(pair_q, k)
    dk_row = mm(pair_k, k) - (beta * growth) * mm(dlow_right, state, 1, 1)
    dkd = tail * mm(ulow, dlow, 1, 1)
    dk_tail = dkd
    dk_col = mm(pair_k, k, 0, 0) + mm(pair_q, q, 0, 0) + dk_tail
    dv = beta * dright
    dbeta = jnp.sum(dright * updates, 1, keepdims=True)
    dlog = jnp.sum(qf * dq + kf * (dk_row - dk_col), 1, keepdims=True)
    dlast = jnp.sum(kf * dk_tail) + jnp.exp(last) * jnp.sum(dend * state.astype(F32))
    dlog_row = jnp.broadcast_to(to_row(dlog, eye), (8, C))
    ddecay_ref[0] = mm(dlog_row, jnp.where(rows >= cols, 1.0, 0.0), precision=lax.Precision.HIGHEST)[:1] + dlast
    dbeta_ref[0] = to_row(dbeta, eye)
    held[...] = mhigh(a_ref[0], dend, 0, 0) + mm(qt_ref[...], do, 0, 0)
    conv_out = conv_ref[...]
    aq, ak, _, inv_q, inv_k = activated(conv_out)
    dk = dk_row + dk_col
    unit_q = aq * inv_q
    unit_k = ak * inv_k
    scale = DK**-0.5
    daq = inv_q * scale * (dq - unit_q * jnp.sum(dq * unit_q, 1, keepdims=True))
    dak = inv_k * (dk - unit_k * jnp.sum(dk * unit_k, 1, keepdims=True))
    dconv = silu_back(conv_out, jnp.concatenate([daq, dak, dv], 1)).astype(BF16).astype(F32)
    dpad[C : C + 8] = dpad[0:8]
    dpad[0:C] = dconv
    draw = sum(
        taps_ref[j : j + 1, :] * dpad[CONV - 1 - j : CONV - 1 - j + C] for j in range(CONV)
    )
    draw_ref[...] = draw.astype(BF16)

    @pl.when(step == 0)
    def _():
        last_ref[...] = draw[C - 8 :]

    @pl.when(step == n - 1)
    def _():
        padded[0:8] = rim_ref[...]
        first_ref[...] = dpad[0:8]

    @pl.when(step < n - 1)
    def _():
        padded[0:8] = before_ref[...][C - 8 :].astype(F32)

    padded[8 : C + 8] = raw_ref[...].astype(F32)
    for j in range(CONV):
        dtaps_ref[j : j + 1, :] += jnp.sum(padded[5 + j : 5 + j + C] * dconv, 0, keepdims=True)


def local_backward(ends, do, q, k, conv, x, p, vt, kt, qt, a, states, decay, beta, raw, rim, taps):
    tokens = do.shape[0]
    n = tokens // C
    back = lambda i: n - 1 - i
    tile = lambda width: pl.BlockSpec((C, width), lambda i: (back(i), 0))
    square = pl.BlockSpec((1, DK, DK), lambda i: (back(i), 0, 0))
    line = pl.BlockSpec((1, 1, C), lambda i: (back(i), 0, 0))
    before = pl.BlockSpec((C, 3 * DK), lambda i: (jnp.maximum(back(i) - 1, 0), 0))
    whole = lambda shape: pl.BlockSpec(shape, lambda i: (0,) * len(shape))
    struct = jax.ShapeDtypeStruct
    return pl.pallas_call(
        backward_kernel,
        grid=(n,),
        in_specs=[whole((DK, DK)), tile(DK), tile(DK), tile(DK), tile(3 * DK), tile(C), tile(C),
                  tile(DK), tile(DK), tile(DK), square, square, line, line,
                  tile(3 * DK), before, whole((8, 3 * DK)), whole((CONV, 3 * DK))],
        out_specs=[tile(3 * DK), line, line, whole((CONV, 3 * DK)), whole((8, 3 * DK)), whole((8, 3 * DK))],
        out_shape=[struct((tokens, 3 * DK), BF16), struct((n, 1, C), F32), struct((n, 1, C), F32),
                   struct((CONV, 3 * DK), F32), struct((8, 3 * DK), F32), struct((8, 3 * DK), F32)],
        scratch_shapes=[pltpu.VMEM((DK, DK), F32), pltpu.VMEM((C + 8, 3 * DK), F32), pltpu.VMEM((C + 8, 3 * DK), F32)],
        compiler_params=pltpu.CompilerParams(vmem_limit_bytes=48 * 2**20),
        name="local_backward",
    )(ends, do, q, k, conv, x, p, vt, kt, qt, a, states, decay, beta, raw, raw, rim, taps)


D = 2048
H = 8
STEP = 7
KEYS = 2048
NPARAM = 55636240
FFP = 768
beta_one = 0.9
beta_two = 0.95
adam_eps = 1e-08
ema_decay = 0.6
rate_matrix = 0.02
rate_vector = 0.5
decay_matrix = 0.1


def group_kernel(z_ref, own_ref, one_ref, two_ref, three_ref, members_ref, total_ref):
    z = z_ref[0]
    for k, ref in enumerate((own_ref, one_ref, two_ref, three_ref)):
        members_ref[lax.rem(z - k + 4, 4)] = ref[...]
    total = members_ref[0].astype(F32)
    for k in range(1, 4):
        member = members_ref[k].astype(F32)
        moved = mhigh(member[:, DK:], total)
        total = jnp.concatenate([moved[:, :DK] + member[:, :DK], moved[:, DK:]], 1)
    total_ref[...] = total.astype(BF16)


def states_kernel(place_ref, own_ref, one_ref, two_ref, three_ref, members_ref, groups_ref, state_ref):
    x = place_ref[0]
    z = place_ref[1]
    for k, ref in enumerate((own_ref, one_ref, two_ref, three_ref)):
        groups_ref[lax.rem(x - k + 4, 4)] = ref[...]
    state_ref[...] = jnp.zeros_like(state_ref)

    def move(ref, index):
        pair = ref[index].astype(F32)
        state_ref[...] = mhigh(pair[:, DK:], state_ref[...]) + pair[:, :DK]

    for k in range(3):
        pl.when(k < x)(partial(move, groups_ref, k))
    for k in range(3):
        pl.when(k < z)(partial(move, members_ref, k))


def group_back_kernel(z_ref, members_ref, own_ref, one_ref, two_ref, three_ref, backs_ref, total_ref):
    z = z_ref[0]
    for k, ref in enumerate((own_ref, one_ref, two_ref, three_ref)):
        backs_ref[lax.rem(z - k + 4, 4)] = ref[...]
    total = backs_ref[3].astype(F32)
    for k in (2, 1, 0):
        total = mhigh(members_ref[k][:, DK:].astype(F32), total, 0, 0) + backs_ref[k].astype(F32)
    total_ref[...] = total.astype(BF16)


def states_back_kernel(place_ref, own_ref, one_ref, two_ref, three_ref, groups_ref, members_ref, backs_ref, state_ref, held):
    x = place_ref[0]
    z = place_ref[1]
    for k, ref in enumerate((own_ref, one_ref, two_ref, three_ref)):
        held[lax.rem(x - k + 4, 4)] = ref[...]
    state_ref[...] = jnp.zeros_like(state_ref)

    def move(ref, back, index):
        transfer = ref[index][:, DK:].astype(F32)
        state_ref[...] = mhigh(transfer, state_ref[...], 0, 0) + back[index].astype(F32)

    for k in (3, 2, 1):
        pl.when(k > x)(partial(move, groups_ref, held, k))
    for k in (3, 2, 1):
        pl.when(k > z)(partial(move, members_ref, backs_ref, k))


SMEM = pl.BlockSpec(memory_space=pltpu.SMEM)
VMEM = pl.BlockSpec(memory_space=pltpu.VMEM)


def small_call(kernel, place, operands, out_shape, scratch=()):
    return pl.pallas_call(
        kernel,
        in_specs=[SMEM] + [VMEM] * len(operands),
        out_specs=[VMEM] * len(out_shape),
        out_shape=out_shape,
        scratch_shapes=list(scratch),
        compiler_params=pltpu.CompilerParams(vmem_limit_bytes=48 * 2**20),
        name=kernel.__name__,
    )(place, *operands)


def shifted(value, shift_of):
    return lax.ppermute(value, "seq", [(i, shift_of(i)) for i in range(16)])


def along_z(value, steps):
    return shifted(value, lambda i: (i // 4) * 4 + (i % 4 + steps) % 4)


def along_x(value, steps):
    return shifted(value, lambda i: (i + 4 * steps) % 16)


def passed_along(value, steps):
    first, last = (max(0, -steps), min(16, 16 - steps))
    return lax.ppermute(value, "seq", [(i, i + steps) for i in range(first, last)])


def split_vectors(vectors):
    offset = 2 * D + DK
    gain_one = vectors[:D]
    gain_two = vectors[D : 2 * D]
    gain_out = vectors[2 * D : offset]
    log_rate = vectors[offset : offset + H]
    rate_bias = vectors[offset + H : offset + 2 * H]
    conv_taps = vectors[offset + 2 * H :].reshape(3, CONV, KEYS)
    return (gain_one, gain_two, gain_out, log_rate, rate_bias, conv_taps)


def rms_rows(values, gain_row):
    inverse = lax.rsqrt(jnp.mean(values * values, -1, keepdims=True) + 1e-05)
    return (values * inverse * gain_row, inverse)


def rms_back(values, inverse, gain_row, grad_normed):
    unit_rows = values * inverse
    grad_gain = jnp.sum(grad_normed * unit_rows, 0)
    grad_unit = grad_normed * gain_row
    grad_values = inverse * (
        grad_unit - unit_rows * jnp.mean(grad_unit * unit_rows, -1, keepdims=True)
    )
    return (grad_values, grad_gain)


def rows_gather(values):
    return lax.all_gather(values, "tp", axis=0, tiled=True)


def rows_reduce(values):
    return lax.psum_scatter(
        values.astype(BF16), "tp", scatter_dimension=0, tiled=True
    ).astype(F32)


def adam_step(weight, gradient, first_old, second_old, average_old, step_rate, decay_rate):
    first_new = beta_one * first_old + (1.0 - beta_one) * gradient
    second_new = beta_two * second_old + (1.0 - beta_two) * gradient * gradient
    direction = (
        first_new
        / (1.0 - beta_one**STEP)
        / (jnp.sqrt(second_new / (1.0 - beta_two**STEP)) + adam_eps)
    )
    weight_new = weight - step_rate * (direction + decay_rate * weight)
    average_new = ema_decay * average_old + (1.0 - ema_decay) * weight_new
    return (weight_new, first_new, second_new, average_new)


def widened(columns, width):
    return jnp.pad(columns, ((0, 0), (0, width - columns.shape[1])))


def dot(a, b, ca, cb, kind=F32):
    return lax.dot_general(a, b, (((ca,), (cb,)), ((), ())), preferred_element_type=F32).astype(kind)


def per_device(
    inputs, cotangent, proj_in, proj_heads, proj_out, proj_mlp, proj_down, vectors,
    first_in, first_heads, first_out, first_mlp, first_down, first_vectors,
    second_in, second_heads, second_out, second_mlp, second_down, second_vectors,
    average_in, average_heads, average_out, average_mlp, average_down, average_vectors,
):
    seq_rank = lax.axis_index("seq")
    tp_rank = lax.axis_index("tp")
    place = jnp.stack([seq_rank // 4, seq_rank % 4]).astype(jnp.int32)
    z_place = place[1:]
    tokens_here = inputs.shape[0] * 8
    chunks = tokens_here // C
    ff = proj_down.shape[0]
    own_in = jnp.concatenate(
        [proj_in[c].astype(BF16) for c in range(4)]
        + [widened(jnp.concatenate([proj_heads[0], proj_heads[1]], 1).astype(BF16), 128)],
        1,
    )
    w_in = lax.all_gather(own_in, "seq", axis=0, tiled=True)
    own_rest = jnp.concatenate(
        [proj_out.astype(BF16).T]
        + [widened(proj_mlp[c].astype(BF16), FFP) for c in range(2)]
        + [widened(proj_down.astype(BF16).T, FFP)],
        1,
    )
    w_rest = lax.all_gather(own_rest, "seq", axis=0, tiled=True)
    w_out = w_rest[:, :DK]
    w_mlp = w_rest[:, DK : DK + 2 * FFP]
    w_down = w_rest[:, DK + 2 * FFP :]
    gain_one, gain_two, gain_out, log_rate, rate_bias, conv_taps = split_vectors(vectors)
    rate_here = jnp.exp(lax.dynamic_slice_in_dim(log_rate, tp_rank, 1))
    bias_here = lax.dynamic_slice_in_dim(rate_bias, tp_rank, 1)
    taps_here = lax.dynamic_slice_in_dim(conv_taps, tp_rank * DK, DK, 2)
    taps_here = jnp.transpose(taps_here, (1, 0, 2)).reshape(CONV, 3 * DK)
    gain_row = gain_out[None]

    start_rows = inputs.astype(F32)
    normed, inverse_one = rms_rows(start_rows, gain_one)
    gathered = rows_gather(normed.astype(BF16))
    projected = dot(gathered, w_in, 1, 0, BF16)
    heads_in = projected[:, 4 * DK : 4 * DK + 2].astype(F32).T
    soft_in = heads_in[0] + bias_here
    decay = (-rate_here * jax.nn.softplus(soft_in)).reshape(chunks, 1, C)
    beta = jax.nn.sigmoid(heads_in[1]).reshape(chunks, 1, C)
    rim = passed_along(projected[tokens_here - 8 :, : 3 * DK], 1).astype(F32)
    q, k, conv, x, p, vt, kt, qt, ol, a, b, total = local_forward(
        projected, rim, taps_here, decay, beta
    )
    pair = total.astype(BF16)
    struct = jax.ShapeDtypeStruct
    pairs = struct((4, DK, 2 * DK), BF16)
    members, group = small_call(
        group_kernel, z_place, [pair] + [along_z(pair, s) for s in (1, 2, 3)],
        [pairs, struct((DK, 2 * DK), BF16)],
    )
    groups, state_in = small_call(
        states_kernel, place, [group] + [along_x(group, s) for s in (1, 2, 3)] + [members],
        [pairs, struct((DK, DK), F32)],
    )
    gated_out, states, o = mixer_output(state_in, a, b, qt, ol, (projected, 3), gain_row)
    attention = rows_reduce(dot(gated_out, w_out, 1, 1, BF16))
    hidden = start_rows + attention
    normed_two, inverse_two = rms_rows(hidden, gain_two)
    gathered_two = rows_gather(normed_two.astype(BF16))
    back_all = rows_gather(cotangent)
    grad_inner = dot(back_all, w_down, 1, 0)
    gate_up = dot(gathered_two, w_mlp, 1, 0)
    gate, upper = gate_up[:, :FFP], gate_up[:, FFP:]
    mlp_sig = jax.nn.sigmoid(gate)
    mlp_act = gate * mlp_sig
    inner_act = (mlp_act * upper).astype(BF16)
    mlp_out = rows_reduce(dot(inner_act, w_down, 1, 1, BF16))
    layer_out = (hidden + mlp_out).astype(BF16)
    grad_gate = grad_inner * upper * mlp_sig * (1.0 + gate * (1.0 - mlp_sig))
    grad_upper = grad_inner * mlp_act
    grad_gu = jnp.concatenate([grad_gate.astype(BF16), grad_upper.astype(BF16)], 1)
    grad_normed_two = rows_reduce(dot(grad_gu, w_mlp, 1, 1, BF16))
    grad_hidden_norm, grad_gain_two = rms_back(hidden, inverse_two, gain_two, grad_normed_two)
    grad_hidden = cotangent.astype(F32) + grad_hidden_norm
    back_hidden = rows_gather(grad_hidden.astype(BF16))
    grad_gated = dot(back_hidden, w_out, 1, 0)
    grad_mixed, grad_gate_raw, grad_gain_out, back_local = output_back(
        grad_gated, o, (projected, 3), gain_row, a, qt
    )
    back_own = back_local.astype(BF16)
    backs, back_group = small_call(
        group_back_kernel, z_place, [members, back_own] + [along_z(back_own, s) for s in (1, 2, 3)],
        [struct((4, DK, DK), BF16), struct((DK, DK), BF16)],
    )
    (state_back,) = small_call(
        states_back_kernel, place,
        [back_group] + [along_x(back_group, s) for s in (1, 2, 3)] + [groups, members, backs],
        [struct((DK, DK), F32)], [pltpu.VMEM((4, DK, DK), BF16)],
    )
    grad_raw, grad_decay, grad_beta, grad_taps, first_rows, last_rows = local_backward(
        state_back, grad_mixed, q, k, conv, x, p, vt, kt, qt, a, states, decay, beta,
        projected, rim, taps_here,
    )
    spill = passed_along(first_rows.astype(BF16), -1).astype(F32)
    ends = jnp.zeros((8, 3 * DK), F32)
    for tap_index in range(3):
        shown = taps_here[tap_index] * spill[: 3 - tap_index]
        ends = ends + jnp.pad(shown, ((5 + tap_index, 0), (0, 0)))
    grad_raw = lax.dynamic_update_slice(
        grad_raw, (last_rows + ends).astype(BF16), (tokens_here - 8, 0)
    )
    grad_decay = grad_decay.reshape(-1)
    grad_soft = grad_decay * -rate_here * jax.nn.sigmoid(soft_in)
    grad_rate = jnp.sum(grad_decay * decay.reshape(-1))
    grad_bias = jnp.sum(grad_soft)
    grad_beta_in = (grad_beta * (1.0 - beta)).reshape(-1)
    grad_heads_in = widened(jnp.stack([grad_soft, grad_beta_in], 1).astype(BF16), 128)
    grad_proj = jnp.concatenate([grad_raw, grad_gate_raw, grad_heads_in], 1)
    grad_normed = rows_reduce(dot(grad_proj, w_in, 1, 1, BF16))
    grad_start_norm, grad_gain_one = rms_back(start_rows, inverse_one, gain_one, grad_normed)
    input_grad = grad_hidden + grad_start_norm

    grad_rest = jnp.concatenate(
        [
            dot(back_hidden, gated_out, 0, 0, BF16),
            dot(gathered_two, grad_gu, 0, 0, BF16),
            dot(back_all, inner_act, 0, 0, BF16),
        ],
        1,
    )
    owned_rest = lax.psum_scatter(grad_rest, "seq", scatter_dimension=0, tiled=True).astype(F32)
    grad_in_w = dot(gathered, grad_proj, 0, 0, BF16)
    owned_first = lax.psum_scatter(grad_in_w, "seq", scatter_dimension=0, tiled=True).astype(F32)
    squares = jnp.sum(owned_rest * owned_rest) + jnp.sum(owned_first * owned_first)

    small = jnp.concatenate(
        [grad_gain_one, grad_gain_two, grad_gain_out[0], squares[None], jnp.zeros((127,), F32),
         grad_taps.reshape(-1), grad_rate[None], grad_bias[None], jnp.zeros((638,), F32)]
    ).reshape(1, 64, 128)
    shared = 2 * D + DK + 128
    over_seq = jnp.sum(
        lax.all_to_all(jnp.broadcast_to(small, (16, 64, 128)), "seq", 0, 0, tiled=True), 0, keepdims=True
    )
    over_tp = lax.all_to_all(
        jnp.broadcast_to(over_seq, (8, 64, 128)), "tp", 0, 0, tiled=True
    ).reshape(8, 8192)
    summed = jnp.sum(over_tp[:, :shared], 0)
    taps_full = over_tp[:, shared : shared + 12 * DK].reshape(8, CONV, 3, DK)
    taps_full = jnp.transpose(taps_full, (2, 1, 0, 3)).reshape(-1)
    small_total = jnp.concatenate(
        [summed[: 2 * D + DK], over_tp[:, shared + 12 * DK], over_tp[:, shared + 12 * DK + 1], taps_full]
    )
    grad_norm = jnp.sqrt(summed[2 * D + DK] + jnp.sum(small_total * small_total))
    factor = jnp.minimum(1.0, 0.5 * math.sqrt(NPARAM) / (grad_norm + 1e-06))
    at = DK + 2 * FFP
    owned_in = jnp.stack([owned_first[:, c * DK : (c + 1) * DK] for c in range(4)])
    owned_heads = jnp.stack([owned_first[:, 4 * DK + c : 4 * DK + c + 1] for c in range(2)])
    owned_out = owned_rest[:, :DK].T
    owned_mlp = jnp.stack([owned_rest[:, DK + c * FFP : DK + c * FFP + ff] for c in range(2)])
    owned_down = owned_rest[:, at : at + ff].T
    new_in = adam_step(proj_in, factor * owned_in, first_in, second_in, average_in, rate_matrix, decay_matrix)
    new_heads = adam_step(proj_heads, factor * owned_heads, first_heads, second_heads, average_heads, rate_matrix, decay_matrix)
    new_out = adam_step(proj_out, factor * owned_out, first_out, second_out, average_out, rate_matrix, decay_matrix)
    new_mlp = adam_step(proj_mlp, factor * owned_mlp, first_mlp, second_mlp, average_mlp, rate_matrix, decay_matrix)
    new_down = adam_step(proj_down, factor * owned_down, first_down, second_down, average_down, rate_matrix, decay_matrix)
    new_small = adam_step(vectors, factor * small_total, first_vectors, second_vectors, average_vectors, rate_vector, 0.0)
    return (layer_out, input_grad, grad_norm, *new_in, *new_heads, *new_out, *new_mlp, *new_down, *new_small)


def solution(mesh):
    rows = P(("seq", "tp"), None)
    wide = P(None, "seq", "tp")
    tall = P("tp", "seq")
    per_kind = (wide, wide, tall, wide, tall, P())
    return jax.shard_map(
        per_device,
        mesh=mesh,
        in_specs=(rows, rows) + per_kind * 4,
        out_specs=(rows, rows, P()) + tuple(kind for kind in per_kind for _ in range(4)),
        check_vma=False,
    )
```

```python
from functools import partial
import math

import jax
import jax.numpy as jnp
from jax import lax
from jax.experimental import pallas as pl
from jax.experimental.layout import Layout, with_layout_constraint
from jax.experimental.pallas import tpu as pltpu
from jax.sharding import PartitionSpec as P

DK = 256
CONV = 4
C = 256
HALF = 128
PAIR = 512
WIDE = 1152
TAIL = 896
HIGH = lax.Precision.HIGH
HIGHEST = lax.Precision.HIGHEST
F32 = jnp.float32
BF16 = jnp.bfloat16
LIMIT = 28 * 2**20
LIMIT_ALL = 60 * 2**20
SCALE = 0.4
TIMES = {
    "forward_kernel": 16, "output_kernel": 4, "output_back_kernel": 4, "backward_kernel": 21, "adam_kernel": 7,
    "mlp_kernel": 7, "mixer_grad_kernel": 4, "token_products": 16, "tail_kernel": 11, "back_kernel": 0, "place_kernel": 5, "out_kernel": 5, "mlp_out_kernel": 12,
}


def cost(microseconds):
    return pl.CostEstimate(flops=0, bytes_accessed=int(microseconds * SCALE * 3.69e6), transcendentals=0)


def mm(a, b, ca=1, cb=0, precision=None):
    return lax.dot_general(
        a, b, (((ca,), (cb,)), ((), ())), precision=precision, preferred_element_type=F32
    )


def mhigh(a, b, ca=1, cb=0):
    return mm(a, b, ca, cb, HIGH)


def sigmoid(v):
    return 1.0 / (1.0 + jnp.exp(-v))


def softplus(v):
    return jnp.maximum(v, 0.0) + jnp.log1p(jnp.exp(-jnp.abs(v)))


def iotas(n):
    rows = lax.broadcasted_iota(jnp.int32, (n, n), 0)
    cols = lax.broadcasted_iota(jnp.int32, (n, n), 1)
    return rows, cols


def to_column(row, eye):
    return jnp.sum(jnp.where(eye, row, 0.0), 1, keepdims=True)


def to_row(column, eye):
    return jnp.sum(jnp.where(eye, column, 0.0), 0, keepdims=True)


def unit_inverses(strict_parts, rows, cols):
    n = rows.shape[0]
    identity = jnp.where(rows == cols, 1.0, 0.0)
    narrow = [part.astype(BF16) for part in strict_parts]
    pairs = rows // 2 == cols // 2
    totals = [identity - jnp.where(pairs, part, 0.0) for part in strict_parts]
    size = 2
    while size < n:
        joint = (rows // (2 * size) == cols // (2 * size)) & (rows // size != cols // size)
        lows = [total.astype(BF16) for total in totals]
        below = [jnp.where(joint, part, jnp.zeros_like(part)) for part in narrow]
        inner = [mm(part, low).astype(BF16) for part, low in zip(below, lows)]
        totals = [total - mm(low, part) for total, low, part in zip(totals, lows, inner)]
        size *= 2
    residuals = [
        identity - total - mhigh(part, total) for part, total in zip(strict_parts, totals)
    ]
    return [total + mhigh(total, residual) for total, residual in zip(totals, residuals)]


def decay_terms(decay_row, rows, cols):
    lower = rows >= cols
    sums = mm(
        jnp.broadcast_to(decay_row, (8, C)), jnp.where(rows <= cols, 1.0, 0.0), precision=HIGHEST
    )[:1]
    column = to_column(sums, rows == cols)
    gap = jnp.where(lower, column - sums, 0.0)
    fading = jnp.where(lower, jnp.exp(gap), 0.0)
    return column, fading


def joined(first_ref, second_ref):
    return jnp.concatenate([first_ref[...], second_ref[...]], 0)


def activated(conv_out):
    act = conv_out * sigmoid(conv_out)
    q, k, v = act[:, :DK], act[:, DK : 2 * DK], act[:, 2 * DK :]
    inv_q = lax.rsqrt(jnp.sum(q * q, 1, keepdims=True) + 1e-06)
    inv_k = lax.rsqrt(jnp.sum(k * k, 1, keepdims=True) + 1e-06)
    return q, k, v, inv_q, inv_k


def gates(scalars_ref, all_columns):
    soft = all_columns[:, 3 * DK : 3 * DK + 1].astype(F32) + scalars_ref[1]
    beta = sigmoid(all_columns[:, 3 * DK + 1 : 3 * DK + 2].astype(F32))
    return soft, -scalars_ref[0] * softplus(soft), beta


def forward_kernel(
    scalars_ref, columns_ref, rim_ref, taps_ref,
    q_ref, k_ref, x_ref, p_ref, vt_ref, kt_ref, qt_ref, ol_ref, a_ref, b_ref, total_ref,
    padded,
):
    step = pl.program_id(0)
    columns = columns_ref[...]

    @pl.when(step == 0)
    def _():
        padded[0:8] = rim_ref[...]

    @pl.when(step > 0)
    def _():
        padded[0:8] = padded[PAIR : PAIR + 8]

    padded[8 : PAIR + 8] = columns[:, : 3 * DK].astype(F32)
    conv_out = sum(taps_ref[j : j + 1, :] * padded[5 + j : 5 + j + PAIR] for j in range(CONV))
    q, k, v, inv_q, inv_k = activated(conv_out)
    q = (q * inv_q * DK**-0.5).astype(BF16)
    k = (k * inv_k).astype(BF16)
    v = v.astype(BF16).astype(F32)
    q_ref[...] = q
    k_ref[...] = k
    rows, cols = iotas(C)
    eye = rows == cols
    _, decay, beta = gates(scalars_ref, columns)
    parts = [slice(h * C, (h + 1) * C) for h in range(PAIR // C)]
    sums = [decay_terms(to_row(decay[part], eye), rows, cols) for part in parts]
    stricts = [
        jnp.where(rows > cols, beta[part] * fading * mm(k[part], k[part], 1, 1), 0.0)
        for part, (_, fading) in zip(parts, sums)
    ]
    inverses = unit_inverses(stricts, rows, cols)
    maps = []
    for h, (part, (column, fading), inverse) in enumerate(zip(parts, sums, inverses)):
        kf = k[part].astype(F32)
        growth = jnp.exp(column)
        last = column[C - 1 : C, :]
        right = jnp.concatenate([beta[part] * v[part], (beta[part] * growth) * kf], 1)
        both = mhigh(inverse, right)
        p = (fading * mm(q[part], k[part], 1, 1)).astype(BF16)
        shared = both.astype(BF16)
        seen = mm(p, shared)
        ol_ref[part] = seen[:, :DK]
        qt_ref[part] = (growth * q[part].astype(F32) - seen[:, DK:]).astype(BF16)
        kd = kf * jnp.exp(last - column)
        ends = mhigh(kd, both, 0, 0)
        a = jnp.where(eye, jnp.exp(last), 0.0) - ends[:, DK:]
        b = ends[:, :DK]
        x_ref[part] = inverse.astype(BF16)
        p_ref[part] = p
        vt_ref[part] = both[:, :DK]
        kt_ref[part] = shared[:, DK:]
        a_ref[h] = a
        b_ref[h] = b
        maps.append((a, b))
    (a, b), (after_a, after_b) = maps
    moved = mhigh(after_a, jnp.concatenate([b, a], 1))
    b = moved[:, :DK] + after_b
    a = moved[:, DK:]

    @pl.when(step == 0)
    def _():
        total_ref[...] = jnp.concatenate([b, a], 1)

    @pl.when(step > 0)
    def _():
        moved = mhigh(a, total_ref[...])
        total_ref[...] = jnp.concatenate([moved[:, :DK] + b, moved[:, DK:]], 1)


struct = jax.ShapeDtypeStruct
SMEM = pl.BlockSpec(memory_space=pltpu.SMEM)
VMEM = pl.BlockSpec(memory_space=pltpu.VMEM)


def whole(shape):
    return pl.BlockSpec(shape, lambda *grid: (0,) * len(shape))


def call(kernel, grid, order, in_specs, out_specs, out_shape, scratch, operands, limit=LIMIT):
    return pl.pallas_call(
        kernel,
        grid_spec=pltpu.PrefetchScalarGridSpec(
            num_scalar_prefetch=1, grid=grid, in_specs=in_specs, out_specs=out_specs, scratch_shapes=scratch
        ),
        out_shape=out_shape,
        compiler_params=pltpu.CompilerParams(vmem_limit_bytes=limit),
        cost_estimate=cost(TIMES[kernel.__name__]),
        name=kernel.__name__,
    )(order, *operands)


def plain_call(kernel, grid, in_specs, out_specs, out_shape, scratch, operands, limit=LIMIT, aliases={}):
    return pl.pallas_call(
        kernel,
        grid=grid,
        in_specs=in_specs,
        out_specs=out_specs,
        out_shape=out_shape,
        scratch_shapes=scratch,
        input_output_aliases=aliases,
        compiler_params=pltpu.CompilerParams(vmem_limit_bytes=limit),
        cost_estimate=cost(TIMES[kernel.__name__]),
        name=kernel.__name__,
    )(*operands)


def local_forward(scalars, columns, rim, taps):
    tokens = columns.shape[0]
    n = tokens // C
    tile = lambda width: pl.BlockSpec((PAIR, width), lambda i: (i, 0))
    square = pl.BlockSpec((PAIR // C, DK, DK), lambda i: (i, 0, 0))
    return plain_call(
        forward_kernel, (tokens // PAIR,),
        [SMEM, tile(WIDE), whole((8, 3 * DK)), whole((CONV, 3 * DK))],
        [tile(DK), tile(DK)] + [tile(C)] * 2 + [tile(DK)] * 4 + [square, square, whole((DK, 2 * DK))],
        [
            pltpu.HBM((tokens, DK), BF16), pltpu.HBM((tokens, DK), BF16),
            pltpu.HBM((tokens, C), BF16), pltpu.HBM((tokens, C), BF16), pltpu.HBM((tokens, DK), F32),
            pltpu.HBM((tokens, DK), BF16), pltpu.HBM((tokens, DK), BF16), pltpu.HBM((tokens, DK), F32),
            pltpu.HBM((n, DK, DK), F32), pltpu.HBM((n, DK, DK), F32), struct((DK, 2 * DK), F32),
        ],
        [pltpu.VMEM((PAIR + 8, 3 * DK), F32)],
        (scalars, columns, rim, taps),
    )


def output_kernel(
    order_ref, state_ref, a_ref, b_ref, qt_ref, ol_ref, gate_ref, gain_ref,
    u_ref, states_ref, o_ref,
    held, rest,
):
    @pl.when((pl.program_id(0) == 0) & (pl.program_id(1) == 0))
    def _():
        held[...] = state_ref[...]

    @pl.when(pl.program_id(1) == 0)
    def _():
        state = held[...]
        low = state.astype(BF16)
        states_ref[0] = low
        o = mm(qt_ref[...], low) + ol_ref[...]
        o_ref[...] = o
        inverse = lax.rsqrt(jnp.mean(o * o, 1, keepdims=True) + 1e-05)
        gate = gate_ref[:, TAIL:].astype(F32)
        u = (o * inverse * gain_ref[...] * (gate * sigmoid(gate))).astype(BF16)
        u_ref[...] = u[:HALF]
        rest[...] = u[HALF:]
        held[...] = mhigh(a_ref[0], state) + b_ref[0]

    @pl.when(pl.program_id(1) == 1)
    def _():
        u_ref[...] = rest[...]


def mixer_output(order, state, a, b, qt, ol, columns, gain):
    tokens = qt.shape[0]
    n = tokens // C
    tile = pl.BlockSpec((C, DK), lambda i, j, order: (i, 0))
    square = pl.BlockSpec((1, DK, DK), lambda i, j, order: (i, 0, 0))
    placed = pl.BlockSpec((HALF, DK), lambda i, j, order: (order[2 * i + j], 0))
    return call(
        output_kernel, (n, 2), order,
        [whole((DK, DK)), square, square, tile, tile,
         pl.BlockSpec((C, WIDE), lambda i, j, order: (i, 0)), whole((1, DK))],
        [placed, square, tile],
        [struct((tokens, DK), BF16), pltpu.HBM((n, DK, DK), BF16), pltpu.HBM((tokens, DK), F32)],
        [pltpu.VMEM((DK, DK), F32), pltpu.VMEM((HALF, DK), BF16)],
        (state, a, b, qt, ol, columns, gain),
    )


def output_back_kernel(
    order_ref, dfirst_ref, dsecond_ref, o_ref, gate_ref, gain_ref, a_ref, qt_ref,
    do_ref, dgate_ref, dgain_ref, back_ref,
    held,
):
    @pl.when(pl.program_id(0) == 0)
    def _():
        held[...] = jnp.zeros_like(held)
        dgain_ref[...] = jnp.zeros_like(dgain_ref)

    o = o_ref[...]
    inverse = lax.rsqrt(jnp.mean(o * o, 1, keepdims=True) + 1e-05)
    unit = o * inverse
    gain = gain_ref[...]
    gate = gate_ref[:, TAIL:].astype(F32)
    sig = sigmoid(gate)
    act = gate * sig
    du = joined(dfirst_ref, dsecond_ref)
    dgate_ref[...] = (du * (unit * gain) * sig * (1.0 + gate * (1.0 - sig))).astype(BF16)
    dm = du * act
    dgain_ref[...] += jnp.sum(dm * unit, 0, keepdims=True)
    e = dm * gain
    do = (inverse * (e - unit * jnp.mean(e * unit, 1, keepdims=True))).astype(BF16)
    do_ref[...] = do
    held[...] = mhigh(a_ref[0], held[...], 0, 0) + mm(qt_ref[...], do, 0, 0)
    back_ref[...] = held[...].astype(BF16)


def output_back(order, du, o, columns, gain, a, qt):
    tokens = o.shape[0]
    n = tokens // C
    back = lambda i: n - 1 - i
    half = lambda h: pl.BlockSpec((HALF, DK), lambda i, order: (order[2 * back(i) + h], 0))
    tile = pl.BlockSpec((C, DK), lambda i, order: (back(i), 0))
    square = pl.BlockSpec((1, DK, DK), lambda i, order: (back(i), 0, 0))
    return call(
        output_back_kernel, (n,), order,
        [half(0), half(1), tile, pl.BlockSpec((C, WIDE), lambda i, order: (back(i), 0)), whole((1, DK)), square, tile],
        [tile, tile, whole((1, DK)), whole((DK, DK))],
        [pltpu.HBM((tokens, DK), BF16), pltpu.HBM((tokens, DK), BF16), struct((1, DK), F32), struct((DK, DK), BF16)],
        [pltpu.VMEM((DK, DK), F32)],
        (du, du, o, columns, gain, a, qt),
    )


def backward_kernel(
    scalars_ref, ends_ref, do_ref, q_ref, k_ref, x_ref, p_ref, vt_ref, kt_ref, qt_ref,
    a_ref, states_ref, columns_ref, before_ref, dgate_ref, rim_ref, taps_ref,
    grad_ref, dtaps_ref, dsmall_ref, opening_ref, closing_ref, spill_ref,
    held, padded, dpad,
):
    step = pl.program_id(0)
    n = pl.num_programs(0)

    @pl.when(step == 0)
    def _():
        held[...] = ends_ref[...]
        dtaps_ref[...] = jnp.zeros_like(dtaps_ref)
        dsmall_ref[...] = jnp.zeros_like(dsmall_ref)
        dpad[...] = jnp.zeros_like(dpad)

    rows, cols = iotas(C)
    eye = rows == cols
    columns = columns_ref[...]
    soft, decay, beta_all = gates(scalars_ref, columns)
    parts = [slice(h * C, (h + 1) * C) for h in range(PAIR // C)]
    dends = [None] * len(parts)
    dend = held[...]
    for h in reversed(range(len(parts))):
        dends[h] = dend
        dend = mhigh(a_ref[h], dend, 0, 0) + mm(qt_ref[parts[h]], do_ref[parts[h]], 0, 0)
    held[...] = dend
    grads = []
    for h, part in enumerate(parts):
        column, fading = decay_terms(to_row(decay[part], eye), rows, cols)
        beta = beta_all[part]
        growth = jnp.exp(column)
        last = column[C - 1 : C, :]
        tail = jnp.exp(last - column)
        q, k, do, p, inverse, state = (
            q_ref[part], k_ref[part], do_ref[part], p_ref[part], x_ref[part], states_ref[h],
        )
        kf = k.astype(F32)
        qf = q.astype(F32)
        kd = (kf * tail).astype(BF16)
        dend = dends[h]
        dlow = dend.astype(BF16)
        updates = vt_ref[part] - mm(kt_ref[part], state)
        ulow = updates.astype(BF16)
        dupdates = mm(p, do, 0, 0) + mm(kd, dlow)
        dright = mm(inverse, dupdates.astype(BF16), 0, 0)
        dlow_right = dright.astype(BF16)
        pair_q = jnp.where(rows >= cols, mm(do, ulow, 1, 1) * fading, 0.0).astype(BF16)
        pair_k = jnp.where(rows > cols, mm(dlow_right, ulow, 1, 1) * (-beta * fading), 0.0).astype(BF16)
        dq = growth * mm(do, state, 1, 1) + mm(pair_q, k)
        dk_row = mm(pair_k, k) - (beta * growth) * mm(dlow_right, state, 1, 1)
        dk_tail = tail * mm(ulow, dlow, 1, 1)
        dk_col = mm(pair_k, k, 0, 0) + mm(pair_q, q, 0, 0) + dk_tail
        dbeta = jnp.sum(dright * updates, 1, keepdims=True)
        dlog = jnp.sum(qf * dq + kf * (dk_row - dk_col), 1, keepdims=True)
        dlast = jnp.sum(kf * dk_tail) + jnp.exp(last) * jnp.sum(dend * state.astype(F32))
        ddecay = (
            mm(jnp.where(rows <= cols, 1.0, 0.0), jnp.broadcast_to(dlog, (C, HALF)), precision=HIGHEST)[:, :1]
            + dlast
        )
        grads.append((dq, dk_row + dk_col, beta * dright, dbeta, ddecay))
    dq, dk, dv, dbeta, ddecay = (jnp.concatenate(pieces, 0) for pieces in zip(*grads))
    dsoft = -scalars_ref[0] * ddecay * sigmoid(soft)
    dbeta_in = dbeta * (1.0 - beta_all)
    lanes = lax.broadcasted_iota(jnp.int32, (PAIR, HALF), 1)
    heads = jnp.where(lanes == 0, dsoft, jnp.where(lanes == 1, dbeta_in, 0.0))
    drate = jnp.sum(ddecay * decay, 0, keepdims=True)
    dbias = jnp.sum(dsoft, 0, keepdims=True)
    dsmall_ref[...] += jnp.where(lanes[:1] == 0, drate, jnp.where(lanes[:1] == 1, dbias, 0.0))
    @pl.when(step == n - 1)
    def _():
        padded[0:8] = rim_ref[...]

    @pl.when(step < n - 1)
    def _():
        padded[0:8] = before_ref[...].astype(F32)[8:, : 3 * DK]

    padded[8 : PAIR + 8] = columns[:, : 3 * DK].astype(F32)
    conv_out = sum(taps_ref[j : j + 1, :] * padded[5 + j : 5 + j + PAIR] for j in range(CONV))
    sig = sigmoid(conv_out)
    act = conv_out * sig
    aq, ak = act[:, :DK], act[:, DK : 2 * DK]
    inv_q = lax.rsqrt(jnp.sum(aq * aq, 1, keepdims=True) + 1e-06)
    inv_k = lax.rsqrt(jnp.sum(ak * ak, 1, keepdims=True) + 1e-06)
    unit_q = aq * inv_q
    unit_k = ak * inv_k
    daq = (inv_q * DK**-0.5) * (dq - unit_q * jnp.sum(dq * unit_q, 1, keepdims=True))
    dak = inv_k * (dk - unit_k * jnp.sum(dk * unit_k, 1, keepdims=True))
    dact = jnp.concatenate([daq, dak, dv], 1)
    dconv = (dact * sig * (1.0 + conv_out * (1.0 - sig))).astype(BF16).astype(F32)
    dpad[PAIR : PAIR + 8] = dpad[0:8]
    dpad[0:PAIR] = dconv
    draw = sum(
        taps_ref[j : j + 1, :] * dpad[CONV - 1 - j : CONV - 1 - j + PAIR] for j in range(CONV)
    )
    grad_ref[...] = jnp.concatenate([draw.astype(BF16), heads.astype(BF16), dgate_ref[...]], 1)

    @pl.when(step == 0)
    def _():
        closing_ref[...] = draw[PAIR - 8 :]

    @pl.when(step == n - 1)
    def _():
        opening_ref[...] = dpad[0:16].astype(BF16)
        place = lax.broadcasted_iota(jnp.int32, (16, TAIL), 0)
        spill = jnp.zeros((16, TAIL), F32)
        for i in range(CONV - 1):
            row = sum(taps_ref[j : j + 1, :] * dpad[i - j : i - j + 1] for j in range(i + 1))
            row = jnp.concatenate([row, jnp.zeros((1, TAIL - 3 * DK), F32)], 1)
            spill = jnp.where(place == 16 - CONV + 1 + i, row, spill)
        spill_ref[...] = spill.astype(BF16)

    for j in range(CONV):
        dtaps_ref[j : j + 1, :] += jnp.sum(padded[5 + j : 5 + j + PAIR] * dconv, 0, keepdims=True)


def local_backward(scalars, ends, do, q, k, x, p, vt, kt, qt, a, states, columns, dgate, rim, taps):
    tokens = do.shape[0]
    n = tokens // PAIR
    back = lambda i: n - 1 - i
    tile = lambda width: pl.BlockSpec((PAIR, width), lambda i: (back(i), 0))
    square = pl.BlockSpec((PAIR // C, DK, DK), lambda i: (back(i), 0, 0))
    before = pl.BlockSpec((16, WIDE), lambda i: (jnp.maximum(back(i) * (PAIR // 16) - 1, 0), 0))
    return plain_call(
        backward_kernel, (n,),
        [SMEM, whole((DK, DK)), tile(DK), tile(DK), tile(DK), tile(C), tile(C),
         tile(DK), tile(DK), tile(DK), square, square, tile(WIDE), before,
         tile(DK), whole((8, 3 * DK)), whole((CONV, 3 * DK))],
        [tile(WIDE), whole((CONV, 3 * DK)), whole((1, HALF)), whole((16, 3 * DK)), whole((8, 3 * DK)), whole((16, TAIL))],
        [struct((tokens, WIDE), BF16), struct((CONV, 3 * DK), F32), struct((1, HALF), F32),
         struct((16, 3 * DK), BF16), struct((8, 3 * DK), F32), struct((16, TAIL), BF16)],
        [pltpu.VMEM((DK, DK), F32), pltpu.VMEM((PAIR + 8, 3 * DK), F32), pltpu.VMEM((PAIR + 8, 3 * DK), F32)],
        (scalars, ends, do, q, k, x, p, vt, kt, qt, a, states, columns, columns, dgate, rim, taps),
        LIMIT_ALL,
    )


def adam_kernel(
    factor_ref, tail_ref, gate_ref, gout_ref, gmlp_ref, gdown_ref, *refs,
):
    factor = factor_ref[0]
    grads = (
        jnp.where(pl.program_id(0) == 3, gate_ref[...], tail_ref[...])[None],
        gout_ref[...],
        gmlp_ref[...],
        gdown_ref[...],
    )
    for m, grad in enumerate(grads):
        olds = [ref[...] for ref in refs[4 * m : 4 * m + 4]]
        news = adam_step(olds[0], factor * grad, *olds[1:], rate_matrix, decay_matrix)
        for ref, new in zip(refs[16 + 4 * m : 20 + 4 * m], news):
            ref[...] = new


def adam_matrices(factor, tail, gate_out, gout, gmlp, gdown, families):
    ff = gdown.shape[0]
    blocks = (
        pl.BlockSpec((1, HALF, DK), lambda i: (i, 0, 0)),
        pl.BlockSpec((DK // 4, HALF), lambda i: (i, 0)),
        pl.BlockSpec((1, ff // 2, HALF), lambda i: (i // 2, i % 2, 0)),
        pl.BlockSpec((ff // 4, HALF), lambda i: (i, 0)),
    )
    specs = [block for block in blocks for _ in range(4)]
    arrays = [array for family in families for array in family]
    outs = plain_call(
        adam_kernel, (4,),
        [SMEM, pl.BlockSpec((HALF, DK), lambda i: (0, jnp.minimum(i, 2))), pl.BlockSpec((HALF, DK), lambda i: (0, 0)),
         *blocks[1:], *specs],
        specs,
        [struct(array.shape, F32) for array in arrays],
        [],
        (factor, tail, gate_out, gout, gmlp, gdown, *arrays),
        LIMIT_ALL,
    )
    return [outs[4 * m : 4 * m + 4] for m in range(4)]


ANY = pl.BlockSpec(memory_space=pl.ANY)


def tie_kernel(*refs):
    pass


def tied(values, *earlier):
    return pl.pallas_call(
        tie_kernel,
        in_specs=[ANY] * (1 + len(earlier)),
        out_specs=ANY,
        out_shape=struct(values.shape, values.dtype),
        input_output_aliases={0: 0},
        cost_estimate=cost(0),
        name="tied",
    )(values, *earlier)


def mlp_kernel(chips, tile, places_ref, *refs):
    row_refs, (w0_ref, w1_ref, back_ref) = refs[: 2 * chips], refs[2 * chips : 2 * chips + 3]
    rows_ref, inner_ref, grad_ref, dn_ref, total, rounded, sems = refs[-7:]
    step = pl.program_id(0)
    rows = jnp.concatenate([ref[...] for ref in row_refs], 0)

    @pl.when(step == 0)
    def _():
        rows_ref[...] = rows

    w0, w1 = w0_ref[...], w1_ref[...]
    gate, upper = mm(rows, w0), mm(rows, w1)
    sig = sigmoid(gate)
    act = gate * sig
    back = back_ref[...]
    dgate = (back * upper * sig * (1.0 + gate * (1.0 - sig))).astype(BF16)
    dupper = (back * act).astype(BF16)
    place = lambda start: pl.ds(pl.multiple_of(start + step * DK, DK), DK)
    inner_ref[:, place(0)] = (act * upper).astype(BF16)
    grad_ref[:, place(0)] = dgate
    grad_ref[:, place(FFP)] = dupper
    dn = mm(dgate, w0, 1, 1) + mm(dupper, w1, 1, 1)

    @pl.when(step == 0)
    def _():
        total[...] = dn

    @pl.when((step > 0) & (step < FFP // DK - 1))
    def _():
        total[...] += dn

    @pl.when(step == FFP // DK - 1)
    def _():
        rounded[...] = (total[...] + dn).astype(BF16)
        copies = []
        for m in range(2 * chips):
            to = pl.ds(pl.multiple_of(places_ref[2 * tile + m] * HALF, HALF), HALF)
            copies.append(
                pltpu.make_async_copy(rounded.at[pl.ds(m * HALF, HALF)], dn_ref.at[to], sems.at[m])
            )
        for copy in copies:
            copy.start()
        for copy in copies:
            copy.wait()


def mlp_tiles(tile, places, pairs, weights, back, buffers):
    chips = len(pairs)
    width = pairs[0][0].shape[1]
    rows = chips * C
    at = tile // chips
    half = pl.BlockSpec((HALF, width), lambda j: (0, 0))
    shapes = [(width, BF16), (FFP, BF16), (2 * FFP, BF16)]
    kernel = partial(mlp_kernel, chips, tile)
    kernel.__name__ = "mlp_kernel"
    return plain_call(
        kernel, (FFP // DK,),
        [SMEM] + [half] * (2 * chips)
        + [pl.BlockSpec((width, DK), lambda j: (0, j)),
           pl.BlockSpec((width, DK), lambda j: (0, FFP // DK + j)),
           pl.BlockSpec((rows, DK), lambda j: (at, j))] + [ANY] * len(buffers),
        [pl.BlockSpec((rows, w), lambda j: (at, 0)) for w, _ in shapes] + [ANY],
        [pltpu.HBM((4 * C, w), kind) for w, kind in shapes] + [pltpu.HBM((4 * C, width), BF16)],
        [pltpu.VMEM((rows, width), F32), pltpu.VMEM((rows, width), BF16), pltpu.SemaphoreType.DMA((2 * chips,))],
        (places, *sum(pairs, ()), weights, weights, back, *buffers),
        LIMIT_ALL, {2 * chips + 4 + m: m for m in range(len(buffers))},
    )


def mixer_grad_kernel(chips, *refs):
    rows_ref, grad_ref, flag_ref = refs[-3:]
    rows = jnp.concatenate([ref[...] for ref in refs[: 2 * chips]], 0)
    rows_ref[...] = rows
    grad_ref[...] = mm(rows, refs[2 * chips][...])
    flag_ref[...] = jnp.zeros_like(flag_ref)


def mixer_grad_tiles(tile, pairs, weights, buffers, earlier=()):
    chips = len(pairs)
    width = pairs[0][0].shape[1]
    rows = chips * C
    at = tile // chips
    half = pl.BlockSpec((HALF, width), lambda i: (0, 0))
    kernel = partial(mixer_grad_kernel, chips)
    kernel.__name__ = "mixer_grad_kernel"
    return plain_call(
        kernel, (1,),
        [half] * (2 * chips) + [pl.BlockSpec((width, DK), lambda i: (0, 0))] + [ANY] * (len(buffers) + len(earlier)),
        [pl.BlockSpec((rows, width), lambda i: (at, 0)), pl.BlockSpec((rows, DK), lambda i: (at, 0)), whole((8, HALF))],
        [pltpu.HBM((4 * C, width), BF16), pltpu.HBM((4 * C, DK), F32), struct((8, HALF), F32)],
        [],
        (*sum(pairs, ()), weights, *buffers, *earlier),
        LIMIT_ALL, {2 * chips + 1 + m: m for m in range(len(buffers))},
    )


def mlp_out_kernel(order_ref, inner_ref, w0_ref, w1_ref, w2_ref, *refs):
    inner = inner_ref[...]
    refs[-1][...] = sum(
        mm(inner[:, m * DK : (m + 1) * DK], ref[...], 1, 1) for m, ref in enumerate((w0_ref, w1_ref, w2_ref))
    ).astype(BF16)


def mlp_products(order, inner, weights, earlier):
    tokens = inner.shape[0]
    width = weights.shape[0]
    column = lambda m: pl.BlockSpec((width, DK), lambda i, order: (0, 1 + m))
    return call(
        mlp_out_kernel, (tokens // HALF,), order,
        [pl.BlockSpec((HALF, FFP), lambda i, order: (order[i], 0)), column(0), column(1), column(2)]
        + [ANY] * len(earlier),
        pl.BlockSpec((HALF, width), lambda i, order: (i, 0)),
        struct((tokens, width), BF16), [], (inner, weights, weights, weights, *earlier), LIMIT_ALL,
    )


def place_kernel(blocks_ref, *refs):
    out_ref = refs[-1]
    for m, ref in enumerate(refs[:-1]):
        out_ref[pl.ds(pl.multiple_of(blocks_ref[m] * HALF, HALF), HALF), :] = ref[...]


def assembled(blocks, pieces):
    width = pieces[0].shape[1]
    rows = len(pieces) * HALF
    return plain_call(
        place_kernel, (1,),
        [SMEM] + [whole((HALF, width))] * len(pieces), whole((rows, width)),
        struct((rows, width), BF16), [], (blocks, *pieces), LIMIT_ALL,
    )


def token_products(pairs, earlier=()):
    counts = [width // DK for _, _, width in pairs]
    starts = [sum(counts[:m]) for m in range(len(pairs))]
    tokens, rows = pairs[0][0].shape

    def kernel(*refs):
        step = pl.program_id(0)
        for m in range(len(pairs)):

            @pl.when((step >= starts[m]) & (step < starts[m] + counts[m]))
            def _():
                refs[-1][...] = mm(refs[2 * m][...], refs[2 * m + 1][...], 0, 0).astype(BF16)

    specs, operands = [], []
    for m, (left, (right, offset), _) in enumerate(pairs):
        place = lambda j, m=m, at=offset // DK: (0, at + jnp.clip(j - starts[m], 0, counts[m] - 1))
        specs += [pl.BlockSpec((tokens, rows), lambda j: (0, 0)), pl.BlockSpec((tokens, DK), place)]
        operands += [left, right]
    kernel.__name__ = "token_products"
    return plain_call(
        kernel, (sum(counts),), specs + [ANY] * len(earlier),
        pl.BlockSpec((rows, DK), lambda j: (0, j)),
        struct((rows, sum(counts) * DK), BF16), [], (*operands, *earlier), LIMIT_ALL,
    )


def back_kernel(order_ref, first_ref, second_ref, right_ref, own_ref, *partner_refs):
    product = mm(joined(first_ref, second_ref), right_ref[...], 1, 1).astype(BF16)
    own_ref[...] = product[:HALF]
    for t, ref in enumerate(partner_refs):

        @pl.when(pl.program_id(0) == t)
        def _():
            ref[...] = product[HALF:]


def product_back(order, left, right):
    tokens, width = left.shape
    rows = right.shape[0]
    tiles = tokens // C
    half = lambda h: pl.BlockSpec((HALF, width), lambda i, order: (order[2 * i + h], 0))
    own, *partners = call(
        back_kernel, (tiles,), order,
        [half(0), half(1), whole((rows, width))],
        [pl.BlockSpec((HALF, rows), lambda i, order: (i, 0))] + [whole((HALF, rows))] * tiles,
        [struct((tokens // 2, rows), BF16)] + [struct((HALF, rows), BF16)] * tiles, [], (left, left, right), LIMIT_ALL,
    )
    return [(own[t * HALF : (t + 1) * HALF], partner) for t, partner in enumerate(partners)]


def tail_kernel(left_ref, right_ref, last_left_ref, last_right_ref, before_ref, spill_ref, out_ref):
    product = mm(left_ref[...], right_ref[...], 0, 0)
    out_ref[:, :TAIL] = (product[:, :TAIL] + mm(before_ref[...], spill_ref[...], 0, 0)).astype(BF16)
    out_ref[:, TAIL:WIDE] = product[:, TAIL:].astype(BF16)
    out_ref[:, WIDE:] = mm(last_left_ref[...], last_right_ref[...], 0, 0).astype(BF16)


def tail_products(left, right, last_left, last_right, before, spill):
    tokens, rows = left.shape
    tall = lambda height: pl.BlockSpec((height, PAIR), lambda j: (0, j))
    return plain_call(
        tail_kernel, (rows // PAIR,),
        [tall(tokens), whole((tokens, WIDE)), tall(tokens), whole((tokens, DK)), tall(16), whole((16, TAIL))],
        pl.BlockSpec((PAIR, WIDE + DK), lambda j: (j, 0)),
        struct((rows, WIDE + DK), BF16), [], (left, right, last_left, last_right, before, spill), LIMIT_ALL,
    )


def out_kernel(left_ref, right_ref, *refs):
    product = mm(left_ref[...], right_ref[...], 1, 1).astype(BF16)
    for t in range(len(refs) // 2):

        @pl.when(pl.program_id(0) == t)
        def _():
            refs[2 * t][...] = product[:HALF]
            refs[2 * t + 1][...] = product[HALF:]


def out_products(left, right):
    tokens = left.shape[0]
    rows = right.shape[0]
    tiles = tokens // C
    outs = plain_call(
        out_kernel, (tiles,),
        [pl.BlockSpec((C, DK), lambda i: (i, 0)), pl.BlockSpec((rows, DK), lambda i: (0, 0))],
        [whole((HALF, rows))] * (2 * tiles), [struct((HALF, rows), BF16)] * (2 * tiles), [], (left, right),
    )
    return [(outs[2 * t], outs[2 * t + 1]) for t in range(tiles)]


D = 2048
H = 8
STEP = 7
KEYS = 2048
NPARAM = 55636240
FFP = 768
beta_one = 0.9
beta_two = 0.95
adam_eps = 1e-08
ema_decay = 0.6
rate_matrix = 0.02
rate_vector = 0.5
decay_matrix = 0.1


def group_kernel(z_ref, own_ref, one_ref, two_ref, three_ref, members_ref, total_ref):
    z = z_ref[0]
    for k, ref in enumerate((own_ref, one_ref, two_ref, three_ref)):
        members_ref[lax.rem(z - k + 4, 4)] = ref[...]
    total = members_ref[0].astype(F32)
    for k in range(1, 4):
        member = members_ref[k].astype(F32)
        moved = mhigh(member[:, DK:], total)
        total = jnp.concatenate([moved[:, :DK] + member[:, :DK], moved[:, DK:]], 1)
    total_ref[...] = total.astype(BF16)


def states_kernel(place_ref, own_ref, one_ref, two_ref, three_ref, members_ref, groups_ref, state_ref):
    x = place_ref[0]
    z = place_ref[1]
    for k, ref in enumerate((own_ref, one_ref, two_ref, three_ref)):
        groups_ref[lax.rem(x - k + 4, 4)] = ref[...]
    state_ref[...] = jnp.zeros_like(state_ref)

    def move(ref, index):
        pair = ref[index].astype(F32)
        state_ref[...] = mhigh(pair[:, DK:], state_ref[...]) + pair[:, :DK]

    for k in range(3):
        pl.when(k < x)(partial(move, groups_ref, k))
    for k in range(3):
        pl.when(k < z)(partial(move, members_ref, k))


def group_back_kernel(place_ref, members_ref, backs_ref, total_ref):
    total = backs_ref[3].astype(F32)
    for k in (2, 1, 0):
        total = mhigh(members_ref[k][:, DK:].astype(F32), total, 0, 0) + backs_ref[k].astype(F32)
    total_ref[...] = total.astype(BF16)


def states_back_kernel(place_ref, groups_ref, group_backs_ref, members_ref, backs_ref, state_ref):
    x = place_ref[0]
    z = place_ref[1]
    state_ref[...] = jnp.zeros_like(state_ref)

    def move(ref, back, index):
        transfer = ref[index][:, DK:].astype(F32)
        state_ref[...] = mhigh(transfer, state_ref[...], 0, 0) + back[index].astype(F32)

    for k in (3, 2, 1):
        pl.when(k > x)(partial(move, groups_ref, group_backs_ref, k))
    for k in (3, 2, 1):
        pl.when(k > z)(partial(move, members_ref, backs_ref, k))


def small_call(kernel, place, operands, out_shape, scratch=()):
    return pl.pallas_call(
        kernel,
        in_specs=[SMEM] + [VMEM] * len(operands),
        out_specs=[VMEM] * len(out_shape),
        out_shape=out_shape,
        scratch_shapes=list(scratch),
        compiler_params=pltpu.CompilerParams(vmem_limit_bytes=LIMIT_ALL),
        cost_estimate=cost(2),
        name=kernel.__name__,
    )(place, *operands)


def after(values, *earlier):
    return lax.optimization_barrier((values, *earlier))[0]


def along_z(value, steps):
    return lax.ppermute(value, "seq", [(i, (i // 4) * 4 + (i + steps) % 4) for i in range(16)])


def along_x(value, steps):
    return lax.ppermute(value, "seq", [(i, (i + 4 * steps) % 16) for i in range(16)])


def along_y(value, steps):
    return lax.ppermute(value, "tp", [(i, (i + 2 * steps) % 8) for i in range(8)])


def swapped(value):
    return lax.ppermute(value, "tp", [(i, i ^ 1) for i in range(8)])


Z_GROUPS = [[4 * x + z for z in range(4)] for x in range(4)]
X_GROUPS = [[4 * x + z for x in range(4)] for z in range(4)]


def shown_to(groups, value):
    copies = jnp.broadcast_to(value, (4, *value.shape))
    return lax.all_to_all(copies, "seq", 0, 0, axis_index_groups=groups, tiled=True)


def passed_along(value, steps):
    first, last = (max(0, -steps), min(16, 16 - steps))
    return lax.ppermute(value, "seq", [(i, i + steps) for i in range(first, last)])


TILES = (1, 3, 0, 2)
PLACES = tuple(TILES.index(d) for d in range(4))
SENDS = (0, 1, 2, -1)


def gathered_rows(rows, together=False):
    ahead, behind = along_y(rows, -1), along_y(rows, 1)
    across = along_y(rows if together else tied(rows + 0, ahead, behind), 2)
    return ahead, behind, rows, across


def gathered_pairs(rows, together=False):
    return [(own, swapped(own)) for own in gathered_rows(rows, together)]


def core_sums(pairs):
    sums = [own.astype(F32) + swapped(partner).astype(F32) for own, partner in pairs]
    return [part.astype(BF16) if d else part for d, part in zip(TILES, sums)]


def arrivals(sums):
    return [along_y(part, SENDS[d]) if d else part for d, part in zip(TILES, sums)]


def chip_sums(parts):
    parts = [part.astype(F32) for part in parts]
    return parts[2] + parts[0] + parts[1] + parts[3]


def split_vectors(vectors):
    offset = 2 * D + DK
    gain_one = vectors[:D]
    gain_two = vectors[D : 2 * D]
    gain_out = vectors[2 * D : offset]
    log_rate = vectors[offset : offset + H]
    rate_bias = vectors[offset + H : offset + 2 * H]
    conv_taps = vectors[offset + 2 * H :].reshape(3, CONV, KEYS)
    return (gain_one, gain_two, gain_out, log_rate, rate_bias, conv_taps)


def rms_rows(values, gain_row):
    inverse = lax.rsqrt(jnp.mean(values * values, -1, keepdims=True) + 1e-05)
    return (values * inverse * gain_row, inverse)


def rms_back(values, inverse, gain_row, grad_normed):
    unit_rows = values * inverse
    grad_gain = jnp.sum(grad_normed * unit_rows, 0)
    grad_unit = grad_normed * gain_row
    grad_values = inverse * (
        grad_unit - unit_rows * jnp.mean(grad_unit * unit_rows, -1, keepdims=True)
    )
    return (grad_values, grad_gain)


def rows_gather(values):
    return lax.all_gather(values, "tp", axis=0, tiled=True)


def rows_reduce(values):
    return lax.psum_scatter(values, "tp", scatter_dimension=0, tiled=True).astype(F32)


def adam_step(weight, gradient, first_old, second_old, average_old, step_rate, decay_rate):
    first_new = beta_one * first_old + (1.0 - beta_one) * gradient
    second_new = beta_two * second_old + (1.0 - beta_two) * gradient * gradient
    direction = (
        first_new
        / (1.0 - beta_one**STEP)
        / (jnp.sqrt(second_new / (1.0 - beta_two**STEP)) + adam_eps)
    )
    weight_new = weight - step_rate * (direction + decay_rate * weight)
    average_new = ema_decay * average_old + (1.0 - ema_decay) * weight_new
    return (weight_new, first_new, second_new, average_new)


def widened(columns, width):
    return jnp.pad(columns, ((0, 0), (0, width - columns.shape[1])))


def dot(a, b, ca, cb, kind=F32):
    return lax.dot_general(a, b, (((ca,), (cb,)), ((), ())), preferred_element_type=F32).astype(kind)


def row_major(values):
    return with_layout_constraint(values, Layout(major_to_minor=(0, 1)))


def seq_gather(values):
    return lax.all_gather(row_major(values), "seq", axis=0, tiled=True)


def seq_reduce(values):
    return lax.psum_scatter(row_major(values), "seq", scatter_dimension=0, tiled=True)


def per_device(
    inputs, cotangent, proj_in, proj_heads, proj_out, proj_mlp, proj_down, vectors,
    first_in, first_heads, first_out, first_mlp, first_down, first_vectors,
    second_in, second_heads, second_out, second_mlp, second_down, second_vectors,
    average_in, average_heads, average_out, average_mlp, average_down, average_vectors,
):
    seq_rank = lax.axis_index("seq")
    tp_rank = lax.axis_index("tp")
    place = jnp.stack([seq_rank // 4, seq_rank % 4]).astype(jnp.int32)
    z_place = place[1:]
    orders = [
        [2 * PLACES[(b // 2 - rank // 2) % 4] + ((b % 2) ^ (rank % 2)) for b in range(8)] for rank in range(8)
    ]
    order = lax.dynamic_index_in_dim(jnp.array(orders, jnp.int32), tp_rank, 0, False)
    inverses = [[row.index(place) for place in range(8)] for row in orders]
    places = lax.dynamic_index_in_dim(jnp.array(inverses, jnp.int32), tp_rank, 0, False)
    tokens_here = inputs.shape[0] * 8
    ff = proj_down.shape[0]
    gain_one, gain_two, gain_out, log_rate, rate_bias, conv_taps = split_vectors(vectors)
    start_rows = inputs.astype(F32)
    normed, inverse_one = rms_rows(start_rows, gain_one)
    tiles_one = sum(gathered_pairs(normed.astype(BF16)), ())
    own_in = jnp.concatenate(
        [proj_in[c].astype(BF16) for c in range(3)]
        + [widened(jnp.concatenate([proj_heads[0], proj_heads[1]], 1).astype(BF16), HALF), proj_in[3].astype(BF16)],
        1,
    )
    w_in = seq_gather(own_in)
    own_ends = jnp.concatenate([proj_out.astype(BF16).T, widened(proj_down.astype(BF16).T, FFP)], 1)
    w_ends = seq_gather(own_ends)
    w_out, w_down = w_ends[:, :DK], w_ends[:, DK:]
    own_mlp = jnp.concatenate([widened(proj_mlp[c].astype(BF16), FFP) for c in range(2)], 1)
    rate_here = jnp.exp(lax.dynamic_slice_in_dim(log_rate, tp_rank, 1))
    bias_here = lax.dynamic_slice_in_dim(rate_bias, tp_rank, 1)
    scalars = jnp.concatenate([rate_here, bias_here])
    taps_here = lax.dynamic_slice_in_dim(conv_taps, tp_rank * DK, DK, 2)
    taps_here = tied(jnp.transpose(taps_here, (1, 0, 2)).reshape(CONV, 3 * DK))
    gain_row = gain_out[None]

    gathered = assembled(places, tiles_one)
    projected = dot(gathered, w_in, 1, 0, BF16)
    cotangent_rows = gathered_rows(tied(cotangent + 0, *tiles_one), True)
    rows_before = passed_along(gathered[tokens_here - 16 :], 1)
    rim = passed_along(projected[tokens_here - 8 :, : 3 * DK], 1).astype(F32)
    q, k, x, p, vt, kt, qt, ol, a, b, total = local_forward(scalars, projected, rim, taps_here)
    pair = tied(total.astype(BF16), *cotangent_rows)
    pairs = struct((4, DK, 2 * DK), BF16)
    members, group = small_call(
        group_kernel, z_place, [pair] + [along_z(pair, s) for s in (1, 2, 3)],
        [pairs, struct((DK, 2 * DK), BF16)],
    )
    groups, state_in = small_call(
        states_kernel, place, [group] + [along_x(group, s) for s in (1, 2, 3)] + [members],
        [pairs, struct((DK, DK), F32)],
    )
    w_mlp = seq_gather(tied(own_mlp, state_in))
    gated_out, states, o = mixer_output(order, state_in, a, b, qt, ol, projected, gain_row)
    cotangent_rows = [tied(rows + 0, gated_out) for rows in cotangent_rows]
    back_all = assembled(
        jnp.arange(8, dtype=jnp.int32), sum(((own, swapped(own)) for own in cotangent_rows), ())
    )
    grad_inner = dot(back_all, w_down, 1, 0)
    attention = chip_sums(arrivals(core_sums(out_products(gated_out, w_ends))))
    hidden = start_rows + attention
    normed_two, inverse_two = rms_rows(hidden, tied(gain_two + 0, grad_inner, rows_before))
    ahead, behind, own, across = gathered_rows(normed_two.astype(BF16))
    buffers = mlp_tiles(2, places, [(own, swapped(own))], w_mlp, grad_inner, ())
    ahead, behind = tied(ahead, buffers[0]), tied(behind, buffers[0])
    buffers = mlp_tiles(0, places, [(ahead, swapped(ahead)), (behind, swapped(behind))], w_mlp, grad_inner, buffers)
    across = tied(across, buffers[0])
    buffers = mlp_tiles(3, places, [(across, swapped(across))], w_mlp, grad_inner, buffers)
    gathered_two, inner_act, grad_gu, partial_two = buffers
    grad_normed_two = rows_reduce(partial_two)
    grad_mlp_down = token_products([(gathered_two, (grad_gu, 0), 2 * FFP), (back_all, (inner_act, 0), FFP)])
    inverse_two = tied(inverse_two, grad_mlp_down)
    grad_hidden_norm, grad_gain_two = rms_back(hidden, inverse_two, gain_two, grad_normed_two)
    grad_hidden = cotangent.astype(F32) + grad_hidden_norm
    hidden_rows = grad_hidden.astype(BF16)
    owned_rest = seq_reduce(tied(grad_mlp_down, hidden_rows))
    *pairs, (across, other) = gathered_pairs(hidden_rows, True)
    *buffers, flag = mixer_grad_tiles(0, pairs, w_ends, ())
    across = tied(across, flag)
    back_hidden, grad_gated, _ = mixer_grad_tiles(3, [(across, swapped(across))], w_ends, buffers)
    grad_mixed, grad_gate_raw, grad_gain_out, back_own = output_back(
        order, grad_gated, o, projected, gain_row, a, qt
    )
    backs = shown_to(Z_GROUPS, back_own)
    (back_group,) = small_call(group_back_kernel, z_place, [members, backs], [struct((DK, DK), BF16)])
    group_backs = shown_to(X_GROUPS, back_group)
    (state_back,) = small_call(
        states_back_kernel, place, [groups, group_backs, members, backs], [struct((DK, DK), F32)]
    )
    grad_proj, grad_taps, grad_small, opening, closing, spill = local_backward(
        scalars, state_back, grad_mixed, q, k, x, p, vt, kt, qt, a, states, projected,
        grad_gate_raw, rim, taps_here,
    )
    grad_tail = tail_products(
        gathered, grad_proj, back_hidden, gated_out, rows_before, tied(spill, owned_rest)
    )
    owned_tail = seq_reduce(grad_tail)
    spill = passed_along(opening, -1).astype(F32)
    ends = jnp.zeros((8, 3 * DK), F32)
    for tap_index in range(3):
        shown = taps_here[tap_index] * spill[: 3 - tap_index]
        ends = ends + jnp.pad(shown, ((5 + tap_index, 0), (0, 0)))
    grad_proj = lax.dynamic_update_slice(
        grad_proj, (closing + ends).astype(BF16), (tokens_here - 8, 0)
    )
    sums_one = core_sums(product_back(tied(places + 0, grad_tail), grad_proj, w_in))
    arrived = arrivals(sums_one)
    grad_normed = chip_sums(arrived)
    mlp_total = rows_reduce(tied(mlp_products(order, inner_act, w_ends, [grad_normed]), owned_tail))
    layer_out = (hidden + mlp_total).astype(BF16)
    grad_start_norm, grad_gain_one = rms_back(start_rows, inverse_one, gain_one, grad_normed)
    input_grad = grad_hidden + grad_start_norm

    owned_rest = owned_rest.astype(F32)
    owned_tail = owned_tail.astype(F32)
    squares = sum(jnp.sum(part * part) for part in (owned_rest, owned_tail))
    small = jnp.concatenate(
        [grad_gain_one, grad_gain_two, grad_gain_out[0], squares[None], jnp.zeros((127,), F32),
         grad_taps.reshape(-1), grad_small[0], jnp.zeros((512,), F32)]
    ).reshape(1, 64, 128)
    shared = 2 * D + DK + 128
    over_seq = jnp.sum(
        lax.all_to_all(jnp.broadcast_to(small, (16, 64, 128)), "seq", 0, 0, tiled=True), 0, keepdims=True
    )
    over_tp = lax.all_to_all(
        jnp.broadcast_to(over_seq, (8, 64, 128)), "tp", 0, 0, tiled=True
    ).reshape(8, 8192)
    summed = jnp.sum(over_tp[:, :shared], 0)
    taps_full = over_tp[:, shared : shared + 12 * DK].reshape(8, CONV, 3, DK)
    taps_full = jnp.transpose(taps_full, (2, 1, 0, 3)).reshape(-1)
    small_total = jnp.concatenate(
        [summed[: 2 * D + DK], over_tp[:, shared + 12 * DK], over_tp[:, shared + 12 * DK + 1], taps_full]
    )
    grad_norm = jnp.sqrt(summed[2 * D + DK] + jnp.sum(small_total * small_total))
    factor = jnp.minimum(1.0, 0.5 * math.sqrt(NPARAM) / (grad_norm + 1e-06))
    owned_heads = jnp.stack([owned_tail[:, 3 * DK + c : 3 * DK + c + 1] for c in range(2)])
    owned_gate = owned_tail[:, TAIL:WIDE]
    owned_out = row_major(owned_tail[:, WIDE:].T)
    turned = row_major(owned_rest.T)
    owned_mlp = jnp.stack([turned[c * FFP : c * FFP + ff] for c in range(2)])
    owned_down = turned[2 * FFP : 2 * FFP + ff]
    flip = lambda *arrays: [jnp.swapaxes(array, 1, 2) for array in arrays]
    new_in, new_out, new_mlp, new_down = adam_matrices(
        factor[None], owned_tail, owned_gate, owned_out, owned_mlp, owned_down,
        (
            (proj_in, first_in, second_in, average_in),
            (proj_out, first_out, second_out, average_out),
            flip(proj_mlp, first_mlp, second_mlp, average_mlp),
            (proj_down, first_down, second_down, average_down),
        ),
    )
    new_mlp = flip(*new_mlp)
    new_heads = adam_step(proj_heads, factor * owned_heads, first_heads, second_heads, average_heads, rate_matrix, decay_matrix)
    new_small = adam_step(vectors, factor * small_total, first_vectors, second_vectors, average_vectors, rate_vector, 0.0)
    return (layer_out, input_grad, grad_norm, *new_in, *new_heads, *new_out, *new_mlp, *new_down, *new_small)


def solution(mesh):
    rows = P(("seq", "tp"), None)
    wide = P(None, "seq", "tp")
    tall = P("tp", "seq")
    per_kind = (wide, wide, tall, wide, tall, P())
    return jax.shard_map(
        per_device,
        mesh=mesh,
        in_specs=(rows, rows) + per_kind * 4,
        out_specs=(rows, rows, P()) + tuple(kind for kind in per_kind for _ in range(4)),
        check_vma=False,
    )
```

```python
from functools import partial
import math

import jax
import jax.numpy as jnp
from jax import lax
from jax.experimental import pallas as pl
from jax.experimental.layout import Layout, with_layout_constraint
from jax.experimental.pallas import tpu as pltpu
from jax.sharding import PartitionSpec as P

DK = 256
CONV = 4
C = 256
HALF = 128
PAIR = 512
WIDE = 1152
TAIL = 896
HIGH = lax.Precision.HIGH
HIGHEST = lax.Precision.HIGHEST
F32 = jnp.float32
BF16 = jnp.bfloat16
LIMIT = 28 * 2**20
LIMIT_ALL = 60 * 2**20
SCALE = 0.4
TIMES = {
    "forward_kernel": 16, "output_kernel": 4, "output_back_kernel": 4, "backward_kernel": 21, "adam_kernel": 7,
    "mlp_kernel": 7, "mixer_grad_kernel": 4, "token_products": 16, "tail_kernel": 8, "back_kernel": 0, "place_kernel": 5, "out_kernel": 5, "sum_kernel": 3, "mlp_out_kernel": 12,
}


def cost(microseconds):
    return pl.CostEstimate(flops=0, bytes_accessed=int(microseconds * SCALE * 3.69e6), transcendentals=0)


def mm(a, b, ca=1, cb=0, precision=None):
    return lax.dot_general(
        a, b, (((ca,), (cb,)), ((), ())), precision=precision, preferred_element_type=F32
    )


def mhigh(a, b, ca=1, cb=0):
    return mm(a, b, ca, cb, HIGH)


def sigmoid(v):
    return 1.0 / (1.0 + jnp.exp(-v))


def softplus(v):
    return jnp.maximum(v, 0.0) + jnp.log1p(jnp.exp(-jnp.abs(v)))


def iotas(n):
    rows = lax.broadcasted_iota(jnp.int32, (n, n), 0)
    cols = lax.broadcasted_iota(jnp.int32, (n, n), 1)
    return rows, cols


def to_column(row, eye):
    return jnp.sum(jnp.where(eye, row, 0.0), 1, keepdims=True)


def to_row(column, eye):
    return jnp.sum(jnp.where(eye, column, 0.0), 0, keepdims=True)


def unit_inverses(strict_parts, rows, cols):
    n = rows.shape[0]
    identity = jnp.where(rows == cols, 1.0, 0.0)
    narrow = [part.astype(BF16) for part in strict_parts]
    pairs = rows // 2 == cols // 2
    totals = [identity - jnp.where(pairs, part, 0.0) for part in strict_parts]
    size = 2
    while size < n:
        joint = (rows // (2 * size) == cols // (2 * size)) & (rows // size != cols // size)
        lows = [total.astype(BF16) for total in totals]
        below = [jnp.where(joint, part, jnp.zeros_like(part)) for part in narrow]
        inner = [mm(part, low).astype(BF16) for part, low in zip(below, lows)]
        totals = [total - mm(low, part) for total, low, part in zip(totals, lows, inner)]
        size *= 2
    residuals = [
        identity - total - mhigh(part, total) for part, total in zip(strict_parts, totals)
    ]
    return [total + mhigh(total, residual) for total, residual in zip(totals, residuals)]


def decay_terms(decay_row, rows, cols):
    lower = rows >= cols
    sums = mm(
        jnp.broadcast_to(decay_row, (8, C)), jnp.where(rows <= cols, 1.0, 0.0), precision=HIGHEST
    )[:1]
    column = to_column(sums, rows == cols)
    gap = jnp.where(lower, column - sums, 0.0)
    fading = jnp.where(lower, jnp.exp(gap), 0.0)
    return column, fading


def joined(first_ref, second_ref):
    return jnp.concatenate([first_ref[...], second_ref[...]], 0)


def activated(conv_out):
    act = conv_out * sigmoid(conv_out)
    q, k, v = act[:, :DK], act[:, DK : 2 * DK], act[:, 2 * DK :]
    inv_q = lax.rsqrt(jnp.sum(q * q, 1, keepdims=True) + 1e-06)
    inv_k = lax.rsqrt(jnp.sum(k * k, 1, keepdims=True) + 1e-06)
    return q, k, v, inv_q, inv_k


def gates(scalars_ref, all_columns):
    soft = all_columns[:, 3 * DK : 3 * DK + 1].astype(F32) + scalars_ref[1]
    beta = sigmoid(all_columns[:, 3 * DK + 1 : 3 * DK + 2].astype(F32))
    return soft, -scalars_ref[0] * softplus(soft), beta


def forward_kernel(
    scalars_ref, columns_ref, rim_ref, taps_ref,
    q_ref, k_ref, x_ref, p_ref, vt_ref, kt_ref, qt_ref, ol_ref, a_ref, b_ref, total_ref,
    padded,
):
    step = pl.program_id(0)
    columns = columns_ref[...]

    @pl.when(step == 0)
    def _():
        padded[0:8] = rim_ref[...]

    @pl.when(step > 0)
    def _():
        padded[0:8] = padded[PAIR : PAIR + 8]

    padded[8 : PAIR + 8] = columns[:, : 3 * DK].astype(F32)
    conv_out = sum(taps_ref[j : j + 1, :] * padded[5 + j : 5 + j + PAIR] for j in range(CONV))
    q, k, v, inv_q, inv_k = activated(conv_out)
    q = (q * inv_q * DK**-0.5).astype(BF16)
    k = (k * inv_k).astype(BF16)
    v = v.astype(BF16).astype(F32)
    q_ref[...] = q
    k_ref[...] = k
    rows, cols = iotas(C)
    eye = rows == cols
    _, decay, beta = gates(scalars_ref, columns)
    parts = [slice(h * C, (h + 1) * C) for h in range(PAIR // C)]
    sums = [decay_terms(to_row(decay[part], eye), rows, cols) for part in parts]
    stricts = [
        jnp.where(rows > cols, beta[part] * fading * mm(k[part], k[part], 1, 1), 0.0)
        for part, (_, fading) in zip(parts, sums)
    ]
    inverses = unit_inverses(stricts, rows, cols)
    maps = []
    for h, (part, (column, fading), inverse) in enumerate(zip(parts, sums, inverses)):
        kf = k[part].astype(F32)
        growth = jnp.exp(column)
        last = column[C - 1 : C, :]
        right = jnp.concatenate([beta[part] * v[part], (beta[part] * growth) * kf], 1)
        both = mhigh(inverse, right)
        p = (fading * mm(q[part], k[part], 1, 1)).astype(BF16)
        shared = both.astype(BF16)
        seen = mm(p, shared)
        ol_ref[part] = seen[:, :DK]
        qt_ref[part] = (growth * q[part].astype(F32) - seen[:, DK:]).astype(BF16)
        kd = kf * jnp.exp(last - column)
        ends = mhigh(kd, both, 0, 0)
        a = jnp.where(eye, jnp.exp(last), 0.0) - ends[:, DK:]
        b = ends[:, :DK]
        x_ref[part] = inverse.astype(BF16)
        p_ref[part] = p
        vt_ref[part] = both[:, :DK]
        kt_ref[part] = shared[:, DK:]
        a_ref[h] = a
        b_ref[h] = b
        maps.append((a, b))
    (a, b), (after_a, after_b) = maps
    moved = mhigh(after_a, jnp.concatenate([b, a], 1))
    b = moved[:, :DK] + after_b
    a = moved[:, DK:]

    @pl.when(step == 0)
    def _():
        total_ref[...] = jnp.concatenate([b, a], 1)

    @pl.when(step > 0)
    def _():
        moved = mhigh(a, total_ref[...])
        total_ref[...] = jnp.concatenate([moved[:, :DK] + b, moved[:, DK:]], 1)


struct = jax.ShapeDtypeStruct
SMEM = pl.BlockSpec(memory_space=pltpu.SMEM)
VMEM = pl.BlockSpec(memory_space=pltpu.VMEM)


def whole(shape):
    return pl.BlockSpec(shape, lambda *grid: (0,) * len(shape))


def call(kernel, grid, order, in_specs, out_specs, out_shape, scratch, operands, limit=LIMIT):
    return pl.pallas_call(
        kernel,
        grid_spec=pltpu.PrefetchScalarGridSpec(
            num_scalar_prefetch=1, grid=grid, in_specs=in_specs, out_specs=out_specs, scratch_shapes=scratch
        ),
        out_shape=out_shape,
        compiler_params=pltpu.CompilerParams(vmem_limit_bytes=limit),
        cost_estimate=cost(TIMES[kernel.__name__]),
        name=kernel.__name__,
    )(order, *operands)


def plain_call(kernel, grid, in_specs, out_specs, out_shape, scratch, operands, limit=LIMIT, aliases={}):
    return pl.pallas_call(
        kernel,
        grid=grid,
        in_specs=in_specs,
        out_specs=out_specs,
        out_shape=out_shape,
        scratch_shapes=scratch,
        input_output_aliases=aliases,
        compiler_params=pltpu.CompilerParams(vmem_limit_bytes=limit),
        cost_estimate=cost(TIMES[kernel.__name__]),
        name=kernel.__name__,
    )(*operands)


def local_forward(scalars, columns, rim, taps):
    tokens = columns.shape[0]
    n = tokens // C
    tile = lambda width: pl.BlockSpec((PAIR, width), lambda i: (i, 0))
    square = pl.BlockSpec((PAIR // C, DK, DK), lambda i: (i, 0, 0))
    return plain_call(
        forward_kernel, (tokens // PAIR,),
        [SMEM, tile(WIDE), whole((8, 3 * DK)), whole((CONV, 3 * DK))],
        [tile(DK), tile(DK)] + [tile(C)] * 2 + [tile(DK)] * 4 + [square, square, whole((DK, 2 * DK))],
        [
            pltpu.HBM((tokens, DK), BF16), pltpu.HBM((tokens, DK), BF16),
            pltpu.HBM((tokens, C), BF16), pltpu.HBM((tokens, C), BF16), pltpu.HBM((tokens, DK), F32),
            pltpu.HBM((tokens, DK), BF16), pltpu.HBM((tokens, DK), BF16), pltpu.HBM((tokens, DK), F32),
            pltpu.HBM((n, DK, DK), F32), pltpu.HBM((n, DK, DK), F32), struct((DK, 2 * DK), F32),
        ],
        [pltpu.VMEM((PAIR + 8, 3 * DK), F32)],
        (scalars, columns, rim, taps),
    )


def output_kernel(
    order_ref, state_ref, a_ref, b_ref, qt_ref, ol_ref, gate_ref, gain_ref,
    u_ref, states_ref, o_ref,
    held, rest,
):
    @pl.when((pl.program_id(0) == 0) & (pl.program_id(1) == 0))
    def _():
        held[...] = state_ref[...]

    @pl.when(pl.program_id(1) == 0)
    def _():
        state = held[...]
        low = state.astype(BF16)
        states_ref[0] = low
        o = mm(qt_ref[...], low) + ol_ref[...]
        o_ref[...] = o
        inverse = lax.rsqrt(jnp.mean(o * o, 1, keepdims=True) + 1e-05)
        gate = gate_ref[:, TAIL:].astype(F32)
        u = (o * inverse * gain_ref[...] * (gate * sigmoid(gate))).astype(BF16)
        u_ref[...] = u[:HALF]
        rest[...] = u[HALF:]
        held[...] = mhigh(a_ref[0], state) + b_ref[0]

    @pl.when(pl.program_id(1) == 1)
    def _():
        u_ref[...] = rest[...]


def mixer_output(order, state, a, b, qt, ol, columns, gain):
    tokens = qt.shape[0]
    n = tokens // C
    tile = pl.BlockSpec((C, DK), lambda i, j, order: (i, 0))
    square = pl.BlockSpec((1, DK, DK), lambda i, j, order: (i, 0, 0))
    placed = pl.BlockSpec((HALF, DK), lambda i, j, order: (order[2 * i + j], 0))
    return call(
        output_kernel, (n, 2), order,
        [whole((DK, DK)), square, square, tile, tile,
         pl.BlockSpec((C, WIDE), lambda i, j, order: (i, 0)), whole((1, DK))],
        [placed, square, tile],
        [struct((tokens, DK), BF16), pltpu.HBM((n, DK, DK), BF16), pltpu.HBM((tokens, DK), F32)],
        [pltpu.VMEM((DK, DK), F32), pltpu.VMEM((HALF, DK), BF16)],
        (state, a, b, qt, ol, columns, gain),
    )


def output_back_kernel(
    order_ref, dfirst_ref, dsecond_ref, o_ref, gate_ref, gain_ref, a_ref, qt_ref,
    do_ref, dgate_ref, dgain_ref, back_ref,
    held,
):
    @pl.when(pl.program_id(0) == 0)
    def _():
        held[...] = jnp.zeros_like(held)
        dgain_ref[...] = jnp.zeros_like(dgain_ref)

    o = o_ref[...]
    inverse = lax.rsqrt(jnp.mean(o * o, 1, keepdims=True) + 1e-05)
    unit = o * inverse
    gain = gain_ref[...]
    gate = gate_ref[:, TAIL:].astype(F32)
    sig = sigmoid(gate)
    act = gate * sig
    du = joined(dfirst_ref, dsecond_ref)
    dgate_ref[...] = (du * (unit * gain) * sig * (1.0 + gate * (1.0 - sig))).astype(BF16)
    dm = du * act
    dgain_ref[...] += jnp.sum(dm * unit, 0, keepdims=True)
    e = dm * gain
    do = (inverse * (e - unit * jnp.mean(e * unit, 1, keepdims=True))).astype(BF16)
    do_ref[...] = do
    held[...] = mhigh(a_ref[0], held[...], 0, 0) + mm(qt_ref[...], do, 0, 0)
    back_ref[...] = held[...].astype(BF16)


def output_back(order, du, o, columns, gain, a, qt):
    tokens = o.shape[0]
    n = tokens // C
    back = lambda i: n - 1 - i
    half = lambda h: pl.BlockSpec((HALF, DK), lambda i, order: (order[2 * back(i) + h], 0))
    tile = pl.BlockSpec((C, DK), lambda i, order: (back(i), 0))
    square = pl.BlockSpec((1, DK, DK), lambda i, order: (back(i), 0, 0))
    return call(
        output_back_kernel, (n,), order,
        [half(0), half(1), tile, pl.BlockSpec((C, WIDE), lambda i, order: (back(i), 0)), whole((1, DK)), square, tile],
        [tile, tile, whole((1, DK)), whole((DK, DK))],
        [pltpu.HBM((tokens, DK), BF16), pltpu.HBM((tokens, DK), BF16), struct((1, DK), F32), struct((DK, DK), BF16)],
        [pltpu.VMEM((DK, DK), F32)],
        (du, du, o, columns, gain, a, qt),
    )


def backward_kernel(
    scalars_ref, ends_ref, do_ref, q_ref, k_ref, x_ref, p_ref, vt_ref, kt_ref, qt_ref,
    a_ref, states_ref, columns_ref, before_ref, dgate_ref, rim_ref, taps_ref,
    grad_ref, dtaps_ref, dsmall_ref, opening_ref, closing_ref, spill_ref,
    held, padded, dpad,
):
    step = pl.program_id(0)
    n = pl.num_programs(0)

    @pl.when(step == 0)
    def _():
        held[...] = ends_ref[...]
        dtaps_ref[...] = jnp.zeros_like(dtaps_ref)
        dsmall_ref[...] = jnp.zeros_like(dsmall_ref)
        dpad[...] = jnp.zeros_like(dpad)

    rows, cols = iotas(C)
    eye = rows == cols
    columns = columns_ref[...]
    soft, decay, beta_all = gates(scalars_ref, columns)
    parts = [slice(h * C, (h + 1) * C) for h in range(PAIR // C)]
    dends = [None] * len(parts)
    dend = held[...]
    for h in reversed(range(len(parts))):
        dends[h] = dend
        dend = mhigh(a_ref[h], dend, 0, 0) + mm(qt_ref[parts[h]], do_ref[parts[h]], 0, 0)
    held[...] = dend
    grads = []
    for h, part in enumerate(parts):
        column, fading = decay_terms(to_row(decay[part], eye), rows, cols)
        beta = beta_all[part]
        growth = jnp.exp(column)
        last = column[C - 1 : C, :]
        tail = jnp.exp(last - column)
        q, k, do, p, inverse, state = (
            q_ref[part], k_ref[part], do_ref[part], p_ref[part], x_ref[part], states_ref[h],
        )
        kf = k.astype(F32)
        qf = q.astype(F32)
        kd = (kf * tail).astype(BF16)
        dend = dends[h]
        dlow = dend.astype(BF16)
        updates = vt_ref[part] - mm(kt_ref[part], state)
        ulow = updates.astype(BF16)
        dupdates = mm(p, do, 0, 0) + mm(kd, dlow)
        dright = mm(inverse, dupdates.astype(BF16), 0, 0)
        dlow_right = dright.astype(BF16)
        pair_q = jnp.where(rows >= cols, mm(do, ulow, 1, 1) * fading, 0.0).astype(BF16)
        pair_k = jnp.where(rows > cols, mm(dlow_right, ulow, 1, 1) * (-beta * fading), 0.0).astype(BF16)
        dq = growth * mm(do, state, 1, 1) + mm(pair_q, k)
        dk_row = mm(pair_k, k) - (beta * growth) * mm(dlow_right, state, 1, 1)
        dk_tail = tail * mm(ulow, dlow, 1, 1)
        dk_col = mm(pair_k, k, 0, 0) + mm(pair_q, q, 0, 0) + dk_tail
        dbeta = jnp.sum(dright * updates, 1, keepdims=True)
        dlog = jnp.sum(qf * dq + kf * (dk_row - dk_col), 1, keepdims=True)
        dlast = jnp.sum(kf * dk_tail) + jnp.exp(last) * jnp.sum(dend * state.astype(F32))
        ddecay = (
            mm(jnp.where(rows <= cols, 1.0, 0.0), jnp.broadcast_to(dlog, (C, HALF)), precision=HIGHEST)[:, :1]
            + dlast
        )
        grads.append((dq, dk_row + dk_col, beta * dright, dbeta, ddecay))
    dq, dk, dv, dbeta, ddecay = (jnp.concatenate(pieces, 0) for pieces in zip(*grads))
    dsoft = -scalars_ref[0] * ddecay * sigmoid(soft)
    dbeta_in = dbeta * (1.0 - beta_all)
    lanes = lax.broadcasted_iota(jnp.int32, (PAIR, HALF), 1)
    heads = jnp.where(lanes == 0, dsoft, jnp.where(lanes == 1, dbeta_in, 0.0))
    drate = jnp.sum(ddecay * decay, 0, keepdims=True)
    dbias = jnp.sum(dsoft, 0, keepdims=True)
    dsmall_ref[...] += jnp.where(lanes[:1] == 0, drate, jnp.where(lanes[:1] == 1, dbias, 0.0))
    @pl.when(step == n - 1)
    def _():
        padded[0:8] = rim_ref[...]

    @pl.when(step < n - 1)
    def _():
        padded[0:8] = before_ref[...].astype(F32)[8:, : 3 * DK]

    padded[8 : PAIR + 8] = columns[:, : 3 * DK].astype(F32)
    conv_out = sum(taps_ref[j : j + 1, :] * padded[5 + j : 5 + j + PAIR] for j in range(CONV))
    sig = sigmoid(conv_out)
    act = conv_out * sig
    aq, ak = act[:, :DK], act[:, DK : 2 * DK]
    inv_q = lax.rsqrt(jnp.sum(aq * aq, 1, keepdims=True) + 1e-06)
    inv_k = lax.rsqrt(jnp.sum(ak * ak, 1, keepdims=True) + 1e-06)
    unit_q = aq * inv_q
    unit_k = ak * inv_k
    daq = (inv_q * DK**-0.5) * (dq - unit_q * jnp.sum(dq * unit_q, 1, keepdims=True))
    dak = inv_k * (dk - unit_k * jnp.sum(dk * unit_k, 1, keepdims=True))
    dact = jnp.concatenate([daq, dak, dv], 1)
    dconv = (dact * sig * (1.0 + conv_out * (1.0 - sig))).astype(BF16).astype(F32)
    dpad[PAIR : PAIR + 8] = dpad[0:8]
    dpad[0:PAIR] = dconv
    draw = sum(
        taps_ref[j : j + 1, :] * dpad[CONV - 1 - j : CONV - 1 - j + PAIR] for j in range(CONV)
    )
    grad_ref[...] = jnp.concatenate([draw.astype(BF16), heads.astype(BF16), dgate_ref[...]], 1)

    @pl.when(step == 0)
    def _():
        closing_ref[...] = draw[PAIR - 8 :]

    @pl.when(step == n - 1)
    def _():
        opening_ref[...] = dpad[0:16].astype(BF16)
        place = lax.broadcasted_iota(jnp.int32, (16, TAIL), 0)
        spill = jnp.zeros((16, TAIL), F32)
        for i in range(CONV - 1):
            row = sum(taps_ref[j : j + 1, :] * dpad[i - j : i - j + 1] for j in range(i + 1))
            row = jnp.concatenate([row, jnp.zeros((1, TAIL - 3 * DK), F32)], 1)
            spill = jnp.where(place == 16 - CONV + 1 + i, row, spill)
        spill_ref[...] = spill.astype(BF16)

    for j in range(CONV):
        dtaps_ref[j : j + 1, :] += jnp.sum(padded[5 + j : 5 + j + PAIR] * dconv, 0, keepdims=True)


def local_backward(scalars, ends, do, q, k, x, p, vt, kt, qt, a, states, columns, dgate, rim, taps):
    tokens = do.shape[0]
    n = tokens // PAIR
    back = lambda i: n - 1 - i
    tile = lambda width: pl.BlockSpec((PAIR, width), lambda i: (back(i), 0))
    square = pl.BlockSpec((PAIR // C, DK, DK), lambda i: (back(i), 0, 0))
    before = pl.BlockSpec((16, WIDE), lambda i: (jnp.maximum(back(i) * (PAIR // 16) - 1, 0), 0))
    return plain_call(
        backward_kernel, (n,),
        [SMEM, whole((DK, DK)), tile(DK), tile(DK), tile(DK), tile(C), tile(C),
         tile(DK), tile(DK), tile(DK), square, square, tile(WIDE), before,
         tile(DK), whole((8, 3 * DK)), whole((CONV, 3 * DK))],
        [tile(WIDE), whole((CONV, 3 * DK)), whole((1, HALF)), whole((16, 3 * DK)), whole((8, 3 * DK)), whole((16, TAIL))],
        [struct((tokens, WIDE), BF16), struct((CONV, 3 * DK), F32), struct((1, HALF), F32),
         struct((16, 3 * DK), BF16), struct((8, 3 * DK), F32), struct((16, TAIL), BF16)],
        [pltpu.VMEM((DK, DK), F32), pltpu.VMEM((PAIR + 8, 3 * DK), F32), pltpu.VMEM((PAIR + 8, 3 * DK), F32)],
        (scalars, ends, do, q, k, x, p, vt, kt, qt, a, states, columns, columns, dgate, rim, taps),
        LIMIT_ALL,
    )


def adam_kernel(
    factor_ref, tail_ref, gate_ref, gout_ref, gmlp_ref, gdown_ref, *refs,
):
    factor = factor_ref[0]
    grads = (
        jnp.where(pl.program_id(0) == 3, gate_ref[...], tail_ref[...])[None],
        gout_ref[...],
        gmlp_ref[...],
        gdown_ref[...],
    )
    for m, grad in enumerate(grads):
        olds = [ref[...] for ref in refs[4 * m : 4 * m + 4]]
        news = adam_step(olds[0], factor * grad, *olds[1:], rate_matrix, decay_matrix)
        for ref, new in zip(refs[16 + 4 * m : 20 + 4 * m], news):
            ref[...] = new


def adam_matrices(factor, tail, gate_out, gout, gmlp, gdown, families):
    ff = gdown.shape[0]
    blocks = (
        pl.BlockSpec((1, HALF, DK), lambda i: (i, 0, 0)),
        pl.BlockSpec((DK // 4, HALF), lambda i: (i, 0)),
        pl.BlockSpec((1, ff // 2, HALF), lambda i: (i // 2, i % 2, 0)),
        pl.BlockSpec((ff // 4, HALF), lambda i: (i, 0)),
    )
    specs = [block for block in blocks for _ in range(4)]
    arrays = [array for family in families for array in family]
    outs = plain_call(
        adam_kernel, (4,),
        [SMEM, pl.BlockSpec((HALF, DK), lambda i: (0, jnp.minimum(i, 2))), pl.BlockSpec((HALF, DK), lambda i: (0, 0)),
         *blocks[1:], *specs],
        specs,
        [struct(array.shape, F32) for array in arrays],
        [],
        (factor, tail, gate_out, gout, gmlp, gdown, *arrays),
        LIMIT_ALL,
    )
    return [outs[4 * m : 4 * m + 4] for m in range(4)]


ANY = pl.BlockSpec(memory_space=pl.ANY)


def tie_kernel(*refs):
    pass


def tied(values, *earlier):
    return pl.pallas_call(
        tie_kernel,
        in_specs=[ANY] * (1 + len(earlier)),
        out_specs=ANY,
        out_shape=struct(values.shape, values.dtype),
        input_output_aliases={0: 0},
        cost_estimate=cost(0),
        name="tied",
    )(values, *earlier)


def mlp_kernel(chips, tile, places_ref, *refs):
    row_refs, (w0_ref, w1_ref, back_ref) = refs[: 2 * chips], refs[2 * chips : 2 * chips + 3]
    rows_ref, inner_ref, grad_ref, dn_ref, total, rounded, sems = refs[-7:]
    step = pl.program_id(0)
    rows = jnp.concatenate([ref[...] for ref in row_refs], 0)

    @pl.when(step == 0)
    def _():
        rows_ref[...] = rows

    w0, w1 = w0_ref[...], w1_ref[...]
    gate, upper = mm(rows, w0), mm(rows, w1)
    sig = sigmoid(gate)
    act = gate * sig
    back = back_ref[...]
    dgate = (back * upper * sig * (1.0 + gate * (1.0 - sig))).astype(BF16)
    dupper = (back * act).astype(BF16)
    place = lambda start: pl.ds(pl.multiple_of(start + step * DK, DK), DK)
    inner_ref[:, place(0)] = (act * upper).astype(BF16)
    grad_ref[:, place(0)] = dgate
    grad_ref[:, place(FFP)] = dupper
    dn = mm(dgate, w0, 1, 1) + mm(dupper, w1, 1, 1)

    @pl.when(step == 0)
    def _():
        total[...] = dn

    @pl.when((step > 0) & (step < FFP // DK - 1))
    def _():
        total[...] += dn

    @pl.when(step == FFP // DK - 1)
    def _():
        rounded[...] = (total[...] + dn).astype(BF16)
        copies = []
        for m in range(2 * chips):
            to = pl.ds(pl.multiple_of(places_ref[2 * tile + m] * HALF, HALF), HALF)
            copies.append(
                pltpu.make_async_copy(rounded.at[pl.ds(m * HALF, HALF)], dn_ref.at[to], sems.at[m])
            )
        for copy in copies:
            copy.start()
        for copy in copies:
            copy.wait()


def mlp_tiles(tile, places, pairs, weights, back, buffers):
    chips = len(pairs)
    width = pairs[0][0].shape[1]
    rows = chips * C
    at = tile // chips
    half = pl.BlockSpec((HALF, width), lambda j: (0, 0))
    shapes = [(width, BF16), (FFP, BF16), (2 * FFP, BF16)]
    kernel = partial(mlp_kernel, chips, tile)
    kernel.__name__ = "mlp_kernel"
    return plain_call(
        kernel, (FFP // DK,),
        [SMEM] + [half] * (2 * chips)
        + [pl.BlockSpec((width, DK), lambda j: (0, j)),
           pl.BlockSpec((width, DK), lambda j: (0, FFP // DK + j)),
           pl.BlockSpec((rows, DK), lambda j: (at, j))] + [ANY] * len(buffers),
        [pl.BlockSpec((rows, w), lambda j: (at, 0)) for w, _ in shapes] + [ANY],
        [pltpu.HBM((4 * C, w), kind) for w, kind in shapes] + [pltpu.HBM((4 * C, width), BF16)],
        [pltpu.VMEM((rows, width), F32), pltpu.VMEM((rows, width), BF16), pltpu.SemaphoreType.DMA((2 * chips,))],
        (places, *sum(pairs, ()), weights, weights, back, *buffers),
        LIMIT_ALL, {2 * chips + 4 + m: m for m in range(len(buffers))},
    )


def mixer_grad_kernel(chips, *refs):
    rows_ref, grad_ref, flag_ref = refs[-3:]
    rows = jnp.concatenate([ref[...] for ref in refs[: 2 * chips]], 0)
    rows_ref[...] = rows
    grad_ref[...] = mm(rows, refs[2 * chips][...])
    flag_ref[...] = jnp.zeros_like(flag_ref)


def mixer_grad_tiles(tile, pairs, weights, buffers, earlier=()):
    chips = len(pairs)
    width = pairs[0][0].shape[1]
    rows = chips * C
    at = tile // chips
    half = pl.BlockSpec((HALF, width), lambda i: (0, 0))
    kernel = partial(mixer_grad_kernel, chips)
    kernel.__name__ = "mixer_grad_kernel"
    return plain_call(
        kernel, (1,),
        [half] * (2 * chips) + [pl.BlockSpec((width, DK), lambda i: (0, 0))] + [ANY] * (len(buffers) + len(earlier)),
        [pl.BlockSpec((rows, width), lambda i: (at, 0)), pl.BlockSpec((rows, DK), lambda i: (at, 0)), whole((8, HALF))],
        [pltpu.HBM((4 * C, width), BF16), pltpu.HBM((4 * C, DK), F32), struct((8, HALF), F32)],
        [],
        (*sum(pairs, ()), weights, *buffers, *earlier),
        LIMIT_ALL, {2 * chips + 1 + m: m for m in range(len(buffers))},
    )


def mlp_out_kernel(order_ref, inner_ref, w0_ref, w1_ref, w2_ref, *refs):
    inner = inner_ref[...]
    refs[-1][...] = sum(
        mm(inner[:, m * DK : (m + 1) * DK], ref[...], 1, 1) for m, ref in enumerate((w0_ref, w1_ref, w2_ref))
    ).astype(BF16)


def mlp_products(order, inner, weights, earlier):
    tokens = inner.shape[0]
    width = weights.shape[0]
    column = lambda m: pl.BlockSpec((width, DK), lambda i, order: (0, 1 + m))
    return call(
        mlp_out_kernel, (tokens // HALF,), order,
        [pl.BlockSpec((HALF, FFP), lambda i, order: (order[i], 0)), column(0), column(1), column(2)]
        + [ANY] * len(earlier),
        pl.BlockSpec((HALF, width), lambda i, order: (i, 0)),
        struct((tokens, width), BF16), [], (inner, weights, weights, weights, *earlier), LIMIT_ALL,
    )


def place_kernel(blocks_ref, *refs):
    out_ref = refs[-1]
    for m, ref in enumerate(refs[:-1]):
        out_ref[pl.ds(pl.multiple_of(blocks_ref[m] * HALF, HALF), HALF), :] = ref[...]


def assembled(blocks, pieces):
    width = pieces[0].shape[1]
    rows = len(pieces) * HALF
    return plain_call(
        place_kernel, (1,),
        [SMEM] + [whole((HALF, width))] * len(pieces), whole((rows, width)),
        struct((rows, width), BF16), [], (blocks, *pieces), LIMIT_ALL,
    )


def token_products(pairs, earlier=()):
    counts = [width // DK for _, _, width in pairs]
    starts = [sum(counts[:m]) for m in range(len(pairs))]
    tokens, rows = pairs[0][0].shape

    def kernel(*refs):
        step = pl.program_id(0)
        for m in range(len(pairs)):

            @pl.when((step >= starts[m]) & (step < starts[m] + counts[m]))
            def _():
                refs[-1][...] = mm(refs[2 * m][...], refs[2 * m + 1][...], 0, 0).astype(BF16)

    specs, operands = [], []
    for m, (left, (right, offset), _) in enumerate(pairs):
        place = lambda j, m=m, at=offset // DK: (0, at + jnp.clip(j - starts[m], 0, counts[m] - 1))
        specs += [pl.BlockSpec((tokens, rows), lambda j: (0, 0)), pl.BlockSpec((tokens, DK), place)]
        operands += [left, right]
    kernel.__name__ = "token_products"
    return plain_call(
        kernel, (sum(counts),), specs + [ANY] * len(earlier),
        pl.BlockSpec((rows, DK), lambda j: (0, j)),
        struct((rows, sum(counts) * DK), BF16), [], (*operands, *earlier), LIMIT_ALL,
    )


def back_kernel(order_ref, first_ref, second_ref, right_ref, *refs):
    halves_out(mm(joined(first_ref, second_ref), right_ref[...], 1, 1), refs)


def product_back(order, left, right):
    tokens, width = left.shape
    rows = right.shape[0]
    tiles = tokens // C
    half = lambda h: pl.BlockSpec((HALF, width), lambda i, order: (order[2 * i + h], 0))
    outs = call(
        back_kernel, (tiles,), order,
        [half(0), half(1), whole((rows, width))],
        [whole((HALF, rows))] * (2 * tiles), [pltpu.HBM((HALF, rows), BF16)] * (2 * tiles), [], (left, left, right), 34 * 2**20,
    )
    return [(outs[2 * t], outs[2 * t + 1]) for t in range(tiles)]


def tail_kernel(left_ref, right_ref, before_ref, spill_ref, out_ref):
    out_ref[...] = (
        mm(left_ref[...], right_ref[...], 0, 0) + mm(before_ref[...], spill_ref[...], 0, 0)
    ).astype(BF16)


def tail_products(left, right, before, spill):
    tokens, rows = left.shape
    tall = lambda height: pl.BlockSpec((height, PAIR), lambda j: (0, j))
    return plain_call(
        tail_kernel, (rows // PAIR,),
        [tall(tokens), whole((tokens, TAIL)), tall(16), whole((16, TAIL))],
        pl.BlockSpec((PAIR, TAIL), lambda j: (j, 0)),
        struct((rows, TAIL), BF16), [], (left, right, before, spill), LIMIT_ALL,
    )


def halves_out(product, refs):
    product = product.astype(BF16)
    for t in range(len(refs) // 2):

        @pl.when(pl.program_id(0) == t)
        def _():
            refs[2 * t][...] = product[:HALF]
            refs[2 * t + 1][...] = product[HALF:]


def out_kernel(left_ref, right_ref, *refs):
    halves_out(mm(left_ref[...], right_ref[...], 1, 1), refs)


def out_products(left, right):
    tokens = left.shape[0]
    rows = right.shape[0]
    tiles = tokens // C
    outs = plain_call(
        out_kernel, (tiles,),
        [pl.BlockSpec((C, DK), lambda i: (i, 0)), pl.BlockSpec((rows, DK), lambda i: (0, 0))],
        [whole((HALF, rows))] * (2 * tiles), [struct((HALF, rows), BF16)] * (2 * tiles), [], (left, right), LIMIT_ALL,
    )
    return [(outs[2 * t], outs[2 * t + 1]) for t in range(tiles)]


def sum_kernel(*refs):
    tiles = len(refs) // 3
    for t in range(tiles):
        out = refs[2 * tiles + t]
        out[...] = (refs[2 * t][...].astype(F32) + refs[2 * t + 1][...].astype(F32)).astype(out.dtype)


def pair_sums(pairs, kinds):
    rows, width = pairs[0][0].shape
    block = pl.BlockSpec((rows, PAIR), lambda i: (0, i))
    return plain_call(
        sum_kernel, (width // PAIR,),
        [block] * (2 * len(pairs)), [block] * len(pairs),
        [struct((rows, width), kind) for kind in kinds], [], sum(pairs, ()), LIMIT_ALL,
    )


D = 2048
H = 8
STEP = 7
KEYS = 2048
NPARAM = 55636240
FFP = 768
beta_one = 0.9
beta_two = 0.95
adam_eps = 1e-08
ema_decay = 0.6
rate_matrix = 0.02
rate_vector = 0.5
decay_matrix = 0.1


def group_kernel(z_ref, own_ref, one_ref, two_ref, three_ref, members_ref, total_ref):
    z = z_ref[0]
    for k, ref in enumerate((own_ref, one_ref, two_ref, three_ref)):
        members_ref[lax.rem(z - k + 4, 4)] = ref[...]
    total = members_ref[0].astype(F32)
    for k in range(1, 4):
        member = members_ref[k].astype(F32)
        moved = mhigh(member[:, DK:], total)
        total = jnp.concatenate([moved[:, :DK] + member[:, :DK], moved[:, DK:]], 1)
    total_ref[...] = total.astype(BF16)


def states_kernel(place_ref, own_ref, one_ref, two_ref, three_ref, members_ref, groups_ref, state_ref):
    x = place_ref[0]
    z = place_ref[1]
    for k, ref in enumerate((own_ref, one_ref, two_ref, three_ref)):
        groups_ref[lax.rem(x - k + 4, 4)] = ref[...]
    state_ref[...] = jnp.zeros_like(state_ref)

    def move(ref, index):
        pair = ref[index].astype(F32)
        state_ref[...] = mhigh(pair[:, DK:], state_ref[...]) + pair[:, :DK]

    for k in range(3):
        pl.when(k < x)(partial(move, groups_ref, k))
    for k in range(3):
        pl.when(k < z)(partial(move, members_ref, k))


def group_back_kernel(place_ref, members_ref, backs_ref, total_ref):
    total = backs_ref[3].astype(F32)
    for k in (2, 1, 0):
        total = mhigh(members_ref[k][:, DK:].astype(F32), total, 0, 0) + backs_ref[k].astype(F32)
    total_ref[...] = total.astype(BF16)


def states_back_kernel(place_ref, groups_ref, group_backs_ref, members_ref, backs_ref, state_ref):
    x = place_ref[0]
    z = place_ref[1]
    state_ref[...] = jnp.zeros_like(state_ref)

    def move(ref, back, index):
        transfer = ref[index][:, DK:].astype(F32)
        state_ref[...] = mhigh(transfer, state_ref[...], 0, 0) + back[index].astype(F32)

    for k in (3, 2, 1):
        pl.when(k > x)(partial(move, groups_ref, group_backs_ref, k))
    for k in (3, 2, 1):
        pl.when(k > z)(partial(move, members_ref, backs_ref, k))


def small_call(kernel, place, operands, out_shape, scratch=()):
    return pl.pallas_call(
        kernel,
        in_specs=[SMEM] + [VMEM] * len(operands),
        out_specs=[VMEM] * len(out_shape),
        out_shape=out_shape,
        scratch_shapes=list(scratch),
        compiler_params=pltpu.CompilerParams(vmem_limit_bytes=LIMIT_ALL),
        cost_estimate=cost(2),
        name=kernel.__name__,
    )(place, *operands)


def after(values, *earlier):
    return lax.optimization_barrier((values, *earlier))[0]


def along_z(value, steps):
    return lax.ppermute(value, "seq", [(i, (i // 4) * 4 + (i + steps) % 4) for i in range(16)])


def along_x(value, steps):
    return lax.ppermute(value, "seq", [(i, (i + 4 * steps) % 16) for i in range(16)])


def along_y(value, steps):
    return lax.ppermute(value, "tp", [(i, (i + 2 * steps) % 8) for i in range(8)])


def swapped(value):
    return lax.ppermute(value, "tp", [(i, i ^ 1) for i in range(8)])


Z_GROUPS = [[4 * x + z for z in range(4)] for x in range(4)]
X_GROUPS = [[4 * x + z for x in range(4)] for z in range(4)]


def shown_to(groups, value):
    copies = jnp.broadcast_to(value, (4, *value.shape))
    return lax.all_to_all(copies, "seq", 0, 0, axis_index_groups=groups, tiled=True)


def passed_along(value, steps):
    first, last = (max(0, -steps), min(16, 16 - steps))
    return lax.ppermute(value, "seq", [(i, i + steps) for i in range(first, last)])


TILES = (1, 3, 0, 2)
PLACES = tuple(TILES.index(d) for d in range(4))
SENDS = (0, 1, 2, -1)


def gathered_rows(rows, together=False):
    ahead, behind = along_y(rows, -1), along_y(rows, 1)
    across = along_y(rows if together else tied(rows + 0, ahead, behind), 2)
    return ahead, behind, rows, across


def gathered_pairs(rows, together=False):
    return [(own, swapped(own)) for own in gathered_rows(rows, together)]


def core_sums(pairs):
    pairs = [(own, swapped(partner)) for own, partner in pairs]
    return pair_sums(pairs, [BF16 if d else F32 for d in TILES])


def arrivals(sums):
    return [along_y(part, SENDS[d]) if d else part for d, part in zip(TILES, sums)]


def chip_sums(parts):
    parts = [part.astype(F32) for part in parts]
    return parts[2] + parts[0] + parts[1] + parts[3]


def split_vectors(vectors):
    offset = 2 * D + DK
    gain_one = vectors[:D]
    gain_two = vectors[D : 2 * D]
    gain_out = vectors[2 * D : offset]
    log_rate = vectors[offset : offset + H]
    rate_bias = vectors[offset + H : offset + 2 * H]
    conv_taps = vectors[offset + 2 * H :].reshape(3, CONV, KEYS)
    return (gain_one, gain_two, gain_out, log_rate, rate_bias, conv_taps)


def rms_rows(values, gain_row):
    inverse = lax.rsqrt(jnp.mean(values * values, -1, keepdims=True) + 1e-05)
    return (values * inverse * gain_row, inverse)


def rms_back(values, inverse, gain_row, grad_normed):
    unit_rows = values * inverse
    grad_gain = jnp.sum(grad_normed * unit_rows, 0)
    grad_unit = grad_normed * gain_row
    grad_values = inverse * (
        grad_unit - unit_rows * jnp.mean(grad_unit * unit_rows, -1, keepdims=True)
    )
    return (grad_values, grad_gain)


def rows_gather(values):
    return lax.all_gather(values, "tp", axis=0, tiled=True)


def rows_reduce(values):
    return lax.psum_scatter(values, "tp", scatter_dimension=0, tiled=True).astype(F32)


def adam_step(weight, gradient, first_old, second_old, average_old, step_rate, decay_rate):
    first_new = beta_one * first_old + (1.0 - beta_one) * gradient
    second_new = beta_two * second_old + (1.0 - beta_two) * gradient * gradient
    direction = (
        first_new
        / (1.0 - beta_one**STEP)
        / (jnp.sqrt(second_new / (1.0 - beta_two**STEP)) + adam_eps)
    )
    weight_new = weight - step_rate * (direction + decay_rate * weight)
    average_new = ema_decay * average_old + (1.0 - ema_decay) * weight_new
    return (weight_new, first_new, second_new, average_new)


def widened(columns, width):
    return jnp.pad(columns, ((0, 0), (0, width - columns.shape[1])))


def dot(a, b, ca, cb, kind=F32):
    return lax.dot_general(a, b, (((ca,), (cb,)), ((), ())), preferred_element_type=F32).astype(kind)


def row_major(values):
    return with_layout_constraint(values, Layout(major_to_minor=(0, 1)))


def seq_gather(values):
    return lax.all_gather(row_major(values), "seq", axis=0, tiled=True)


def seq_reduce(values):
    return lax.psum_scatter(row_major(values), "seq", scatter_dimension=0, tiled=True)


def per_device(
    inputs, cotangent, proj_in, proj_heads, proj_out, proj_mlp, proj_down, vectors,
    first_in, first_heads, first_out, first_mlp, first_down, first_vectors,
    second_in, second_heads, second_out, second_mlp, second_down, second_vectors,
    average_in, average_heads, average_out, average_mlp, average_down, average_vectors,
):
    seq_rank = lax.axis_index("seq")
    tp_rank = lax.axis_index("tp")
    place = jnp.stack([seq_rank // 4, seq_rank % 4]).astype(jnp.int32)
    z_place = place[1:]
    orders = [
        [2 * PLACES[(b // 2 - rank // 2) % 4] + ((b % 2) ^ (rank % 2)) for b in range(8)] for rank in range(8)
    ]
    order = lax.dynamic_index_in_dim(jnp.array(orders, jnp.int32), tp_rank, 0, False)
    inverses = [[row.index(place) for place in range(8)] for row in orders]
    places = lax.dynamic_index_in_dim(jnp.array(inverses, jnp.int32), tp_rank, 0, False)
    tokens_here = inputs.shape[0] * 8
    ff = proj_down.shape[0]
    gain_one, gain_two, gain_out, log_rate, rate_bias, conv_taps = split_vectors(vectors)
    start_rows = inputs.astype(F32)
    normed, inverse_one = rms_rows(start_rows, gain_one)
    tiles_one = sum(gathered_pairs(normed.astype(BF16)), ())
    own_in = jnp.concatenate(
        [proj_in[c].astype(BF16) for c in range(3)]
        + [widened(jnp.concatenate([proj_heads[0], proj_heads[1]], 1).astype(BF16), HALF), proj_in[3].astype(BF16)],
        1,
    )
    w_in = seq_gather(own_in)
    own_ends = jnp.concatenate([proj_out.astype(BF16).T, widened(proj_down.astype(BF16).T, FFP)], 1)
    w_ends = seq_gather(own_ends)
    w_out, w_down = w_ends[:, :DK], w_ends[:, DK:]
    own_mlp = jnp.concatenate([widened(proj_mlp[c].astype(BF16), FFP) for c in range(2)], 1)
    rate_here = jnp.exp(lax.dynamic_slice_in_dim(log_rate, tp_rank, 1))
    bias_here = lax.dynamic_slice_in_dim(rate_bias, tp_rank, 1)
    scalars = jnp.concatenate([rate_here, bias_here])
    taps_here = lax.dynamic_slice_in_dim(conv_taps, tp_rank * DK, DK, 2)
    taps_here = tied(jnp.transpose(taps_here, (1, 0, 2)).reshape(CONV, 3 * DK))
    gain_row = gain_out[None]

    gathered = assembled(places, tiles_one)
    projected = dot(gathered, w_in, 1, 0, BF16)
    cotangent_rows = gathered_rows(tied(cotangent + 0, *tiles_one), True)
    rows_before = passed_along(gathered[tokens_here - 16 :], 1)
    rim = dot(rows_before, w_in, 1, 0, BF16)[8:, : 3 * DK].astype(F32)
    q, k, x, p, vt, kt, qt, ol, a, b, total = local_forward(scalars, projected, rim, taps_here)
    pair = tied(total.astype(BF16), *cotangent_rows)
    pairs = struct((4, DK, 2 * DK), BF16)
    members, group = small_call(
        group_kernel, z_place, [pair] + [along_z(pair, s) for s in (1, 2, 3)],
        [pairs, struct((DK, 2 * DK), BF16)],
    )
    groups, state_in = small_call(
        states_kernel, place, [group] + [along_x(group, s) for s in (1, 2, 3)] + [members],
        [pairs, struct((DK, DK), F32)],
    )
    w_mlp = seq_gather(tied(own_mlp, state_in))
    gated_out, states, o = mixer_output(order, state_in, a, b, qt, ol, projected, gain_row)
    cotangent_rows = [tied(rows + 0, gated_out) for rows in cotangent_rows]
    back_all = assembled(
        jnp.arange(8, dtype=jnp.int32), sum(((own, swapped(own)) for own in cotangent_rows), ())
    )
    grad_inner = dot(back_all, w_down, 1, 0)
    attention = chip_sums(arrivals(core_sums(out_products(gated_out, w_ends))))
    hidden = start_rows + attention
    normed_two, inverse_two = rms_rows(hidden, tied(gain_two + 0, grad_inner))
    ahead, behind, own, across = gathered_rows(normed_two.astype(BF16))
    buffers = mlp_tiles(2, places, [(own, swapped(own))], w_mlp, grad_inner, ())
    ahead, behind = tied(ahead, buffers[0]), tied(behind, buffers[0])
    buffers = mlp_tiles(0, places, [(ahead, swapped(ahead)), (behind, swapped(behind))], w_mlp, grad_inner, buffers)
    across = tied(across, buffers[0])
    buffers = mlp_tiles(3, places, [(across, swapped(across))], w_mlp, grad_inner, buffers)
    gathered_two, inner_act, grad_gu, partial_two = buffers
    grad_normed_two = rows_reduce(partial_two)
    grad_mlp_down = token_products([(gathered_two, (grad_gu, 0), 2 * FFP), (back_all, (inner_act, 0), FFP)])
    mlp_out = mlp_products(order, inner_act, w_ends, ())
    inverse_two = tied(inverse_two, grad_mlp_down, mlp_out)
    grad_hidden_norm, grad_gain_two = rms_back(hidden, inverse_two, gain_two, grad_normed_two)
    grad_hidden = cotangent.astype(F32) + grad_hidden_norm
    hidden_rows = grad_hidden.astype(BF16)
    owned_rest = seq_reduce(tied(grad_mlp_down, hidden_rows))
    *pairs, (across, other) = gathered_pairs(hidden_rows, True)
    *buffers, flag = mixer_grad_tiles(0, pairs, w_ends, ())
    across = tied(across, flag)
    back_hidden, grad_gated, _ = mixer_grad_tiles(3, [(across, swapped(across))], w_ends, buffers)
    grad_mixed, grad_gate_raw, grad_gain_out, back_own = output_back(
        order, grad_gated, o, projected, gain_row, a, qt
    )
    backs = shown_to(Z_GROUPS, back_own)
    (back_group,) = small_call(group_back_kernel, z_place, [members, backs], [struct((DK, DK), BF16)])
    group_backs = shown_to(X_GROUPS, back_group)
    grad_gate_out = token_products(
        [(gathered, (grad_gate_raw, 0), DK), (back_hidden, (gated_out, 0), DK)], (backs,)
    )
    (state_back,) = small_call(
        states_back_kernel, tied(place + 0, grad_gate_out), [groups, group_backs, members, backs], [struct((DK, DK), F32)]
    )
    grad_proj, grad_taps, grad_small, opening, closing, spill = local_backward(
        scalars, state_back, grad_mixed, q, k, x, p, vt, kt, qt, a, states, projected,
        grad_gate_raw, rim, taps_here,
    )
    gate_out_parts = lax.all_to_all(tied(grad_gate_out, state_back), "seq", 0, 0, tiled=True)
    mlp_total = rows_reduce(tied(mlp_out, owned_rest))
    layer_out = (hidden + mlp_total).astype(BF16)
    grad_tail = tail_products(gathered, grad_proj, rows_before, spill)
    received = passed_along(opening, -1)
    grad_tail = tied(grad_tail, received, gate_out_parts)
    tail_parts = lax.all_to_all(grad_tail, "seq", 0, 0, tiled=True)
    spill = received.astype(F32)
    ends = jnp.zeros((8, 3 * DK), F32)
    for tap_index in range(3):
        shown = taps_here[tap_index] * spill[: 3 - tap_index]
        ends = ends + jnp.pad(shown, ((5 + tap_index, 0), (0, 0)))
    grad_proj = lax.dynamic_update_slice(
        grad_proj, (closing + ends).astype(BF16), (tokens_here - 8, 0)
    )
    sums_one = core_sums(product_back(tied(places + 0, grad_tail), grad_proj, w_in))
    summed_parts = lambda parts: jnp.sum(parts.reshape(16, -1, parts.shape[1]).astype(F32), 0)
    owned_tail = summed_parts(tied(tail_parts, *sums_one))
    owned_gate_out = summed_parts(gate_out_parts)
    arrived = arrivals(sums_one)
    grad_normed = chip_sums(arrived)
    grad_start_norm, grad_gain_one = rms_back(start_rows, inverse_one, gain_one, grad_normed)
    input_grad = grad_hidden + grad_start_norm

    owned_rest = owned_rest.astype(F32)
    lanes = lambda part: jnp.sum((part * part).reshape(part.shape[0], -1, 128), (0, 1))
    squares = lanes(owned_rest) + lanes(owned_gate_out) + lanes(owned_tail)
    small = jnp.concatenate(
        [grad_gain_one, grad_gain_two, grad_gain_out[0], squares,
         grad_taps.reshape(-1), grad_small[0], jnp.zeros((512,), F32)]
    ).reshape(1, 64, 128)
    shared = 2 * D + DK + 128
    over_seq = jnp.sum(
        lax.all_to_all(jnp.broadcast_to(small, (16, 64, 128)), "seq", 0, 0, tiled=True), 0, keepdims=True
    )
    over_tp = lax.all_to_all(
        jnp.broadcast_to(over_seq, (8, 64, 128)), "tp", 0, 0, tiled=True
    ).reshape(8, 8192)
    summed = jnp.sum(over_tp[:, :shared], 0)
    taps_full = over_tp[:, shared : shared + 12 * DK].reshape(8, CONV, 3, DK)
    taps_full = jnp.transpose(taps_full, (2, 1, 0, 3)).reshape(-1)
    small_total = jnp.concatenate(
        [summed[: 2 * D + DK], over_tp[:, shared + 12 * DK], over_tp[:, shared + 12 * DK + 1], taps_full]
    )
    grad_norm = jnp.sqrt(jnp.sum(summed[2 * D + DK :]) + jnp.sum(small_total * small_total))
    factor = jnp.minimum(1.0, 0.5 * math.sqrt(NPARAM) / (grad_norm + 1e-06))
    owned_heads = jnp.stack([owned_tail[:, 3 * DK + c : 3 * DK + c + 1] for c in range(2)])
    owned_out = row_major(owned_gate_out[:, DK:].T)
    turned = row_major(owned_rest.T)
    owned_mlp = jnp.stack([turned[c * FFP : c * FFP + ff] for c in range(2)])
    owned_down = turned[2 * FFP : 2 * FFP + ff]
    flip = lambda *arrays: [jnp.swapaxes(array, 1, 2) for array in arrays]
    new_in, new_out, new_mlp, new_down = adam_matrices(
        factor[None], owned_tail, owned_gate_out, owned_out, owned_mlp, owned_down,
        (
            (proj_in, first_in, second_in, average_in),
            (proj_out, first_out, second_out, average_out),
            flip(proj_mlp, first_mlp, second_mlp, average_mlp),
            (proj_down, first_down, second_down, average_down),
        ),
    )
    new_mlp = flip(*new_mlp)
    new_heads = adam_step(proj_heads, factor * owned_heads, first_heads, second_heads, average_heads, rate_matrix, decay_matrix)
    new_small = adam_step(vectors, factor * small_total, first_vectors, second_vectors, average_vectors, rate_vector, 0.0)
    return (layer_out, input_grad, grad_norm, *new_in, *new_heads, *new_out, *new_mlp, *new_down, *new_small)


def solution(mesh):
    rows = P(("seq", "tp"), None)
    wide = P(None, "seq", "tp")
    tall = P("tp", "seq")
    per_kind = (wide, wide, tall, wide, tall, P())
    return jax.shard_map(
        per_device,
        mesh=mesh,
        in_specs=(rows, rows) + per_kind * 4,
        out_specs=(rows, rows, P()) + tuple(kind for kind in per_kind for _ in range(4)),
        check_vma=False,
    )
```
